256 devices in a mesh: grp: 8 (over x, core), shard: 32 (over y, z).
Axes of the slice: x: 4, y: 4, z: 8, core: 2. Of those that a mesh axis runs over, the one named last changes fastest.
Arguments:
- features: bfloat16 [262144, 1280], P(('grp', 'shard')), parts along dimension 0
- norm_gain: float32 [1280], replicated, may hold values from 0.1 to 1.9
- norm_shift: float32 [1280], replicated, may hold values from -3 to 3
- merge_weight: bfloat16 [2560, 1280], P('shard'), may hold values from -0.125 to 0.125
- out_weight: bfloat16 [1280, 1280], P('shard'), may hold values from -0.15625 to 0.15625
- corr_src: int32 [2048, 3], P('grp'), parts along dimension 0, may hold values from 0 to 255, as said below
- corr_count: int32 [2048], P('grp'), parts along dimension 0, may hold values from 1 to 3
Outputs:
- block_out: bfloat16 [262144, 1280], P(('grp', 'shard')), parts along dimension 0
The draws below stay inside these ranges and needn't reach their ends.
There are 8 independent parts, one for each index of `grp`. The reference program is written for one: setup_inputs(seed, part) draws one part's arguments, and reference() takes and returns one part's arrays. A program takes and returns all parts, laid end to end along the dimension named above; an argument that names none is the same for every part. Nothing has to cross between parts.
Inputs may be any that keep to these rules, and one draw needn't show every extreme that they name: `corr_src`: every source block belongs to another view than the block that lists it. Over all 24 slots of one view's blocks (valid or not), the source blocks of any one other view number at most 1, and that number is reached.
All inputs are finite; a program needn't handle non-finite values.
Results may differ from the reference program's by a relative error of at most 0.0018.
Values may be sent and summed in bfloat16 or wider, within the bound.
A program may use at most 128 MiB of HBM per device.

```python
import math
import jax
import jax.numpy as jnp
from jax import lax

C = 1280
GROUPS = 32
IMG = 32
BLOCK = 128
LIST = 3
BLK_DEV = 8
TOKENS = 32768
BLOCKS = 256
N_SHARD = 32


def draw_features(key, part):
    key = jax.random.fold_in(key, 3)
    keys = jax.random.split(key, 3)
    base = jax.random.normal(keys[0], (TOKENS, C), jnp.float32)
    view_low = 0.5
    view_high = 2.0
    channel = jnp.exp(jax.random.uniform(keys[1], (C,), jnp.float32, math.log(0.3), math.log(3.0)))
    view_scale = jnp.exp(jax.random.uniform(keys[2], (N_SHARD,), jnp.float32, math.log(view_low), math.log(view_high)))
    block_index = jnp.arange(BLOCKS, dtype=jnp.int32)
    ramp = 1.0 + 2.0 * (block_index % BLK_DEV).astype(jnp.float32) / float(max(BLK_DEV - 1, 1))
    block_scale = view_scale[block_index // BLK_DEV] * ramp
    row_scale = jnp.repeat(block_scale, BLOCK)
    return (base * channel[None, :] * row_scale[:, None]).astype(jnp.bfloat16)


def draw_corr_src(key, part):
    key = jax.random.fold_in(key, 7)
    keys = jax.random.split(key, 3)
    views = BLOCKS // BLK_DEV
    entries = BLK_DEV * LIST
    offsets = jax.random.randint(keys[0], (views,), 0, views - 1, dtype=jnp.int32)
    orders = jax.vmap(lambda single: jax.random.permutation(single, entries))(jax.random.split(keys[1], views))
    receiver = jnp.arange(views, dtype=jnp.int32)[:, None]
    step_away = 1 + (offsets[:, None] + orders.astype(jnp.int32)) % (views - 1)
    sender = (receiver + step_away) % views
    local_block = jax.random.randint(keys[2], (views, entries), 0, BLK_DEV, dtype=jnp.int32)
    return (sender * BLK_DEV + local_block).reshape(BLOCKS, LIST).astype(jnp.int32)


def plant(values, own_key, smallest, largest):
    shape = values.shape
    index_at = [jax.random.randint(jax.random.fold_in(own_key, axis), (), 0, shape[axis]) for axis in range(len(shape))]
    values = values.at[tuple(index_at)].set(smallest)
    longest = shape.index(max(shape))
    index_at[longest] = (index_at[longest] + 1) % shape[longest]
    return values.at[tuple(index_at)].set(largest)


def block_levels(key, extent, shards, low, largest):
    level, own = 1.0, jax.random.fold_in(key, 6)
    for dim, shards_of in shards:
        heights = jnp.exp(jax.random.uniform(jax.random.fold_in(own, dim), (shards_of,), jnp.float32, low / len(shards), largest / len(shards)))
        level = level * jnp.repeat(heights, extent[dim] // shards_of).reshape([-1 if axis == dim else 1 for axis in range(len(extent))])
    return level


def centred(rng, dims, scale, bound, pieces=(), held_as=jnp.bfloat16):
    drawn = jax.random.normal(rng, dims, jnp.float32) * scale
    if len(pieces) > 0:
        drawn = block_levels(rng, dims, pieces, -0.22, 0.18) * drawn
    return jnp.clip(drawn, min=-bound, max=bound).astype(held_as)


def setup_inputs(seed: int = 0, part: int = 0) -> dict:
    streams_of = jax.random.split(jax.random.key(seed), 8)
    part_keys = jax.random.split(jax.random.fold_in(streams_of[7], part), 8)
    features = draw_features(jax.random.fold_in(jax.random.fold_in(streams_of[7], part), 71), part)
    norm_gain = jnp.clip(1.0 + 0.18 * jax.random.normal(streams_of[1], (C,), jnp.float32), 0.1, 1.9)
    norm_shift = centred(streams_of[2], (C,), 0.5, 3.0, (), jnp.float32)
    merge_weight = centred(streams_of[3], (2 * C, C), (2 * C) ** -0.5, 0.125, ((0, 32),))
    out_weight = centred(streams_of[4], (C, C), C ** -0.5, 0.15625, ((0, 32),))
    corr_src = draw_corr_src(jax.random.fold_in(jax.random.fold_in(streams_of[7], part), 71), part)
    corr_count = plant(jax.random.randint(part_keys[6], (BLOCKS,), 1, LIST + 1), jax.random.fold_in(part_keys[6], 1), 1, LIST).astype(jnp.int32)
    return {"features": features, "norm_gain": norm_gain, "norm_shift": norm_shift, "merge_weight": merge_weight, "out_weight": out_weight, "corr_src": corr_src, "corr_count": corr_count}


def group_norm(values):
    grouped = values.reshape(N_SHARD, IMG * IMG, GROUPS, C // GROUPS)
    members = float(IMG * IMG * (C // GROUPS))
    average = lax.optimization_barrier(jnp.sum(grouped, axis=(1, 3), keepdims=True)) / members
    centered = grouped - average
    variance = lax.optimization_barrier(jnp.sum(centered * centered, axis=(1, 3), keepdims=True)) / members
    return (centered * lax.rsqrt(variance + 1e-05)).reshape(TOKENS, C)

def reference(features, norm_gain, norm_shift, merge_weight, out_weight, corr_src, corr_count):
    inputs = features.astype(jnp.float32)
    hidden = jax.nn.silu(group_norm(inputs) * norm_gain + norm_shift).astype(jnp.bfloat16)
    hidden_blocks = hidden.reshape(BLOCKS, BLOCK, C)
    valid = (jnp.arange(LIST, dtype=jnp.int32)[None, :] < corr_count[:, None]).astype(jnp.float32)
    summed = jnp.zeros((BLOCKS, BLOCK, C), jnp.float32)
    for position in range(LIST):
        picked = jnp.take(hidden_blocks, corr_src[:, position], axis=0)
        summed = summed + picked.astype(jnp.float32) * valid[:, position, None, None]
    divisor = corr_count.astype(jnp.float32)[:, None, None]
    epipolar = (summed / divisor).astype(jnp.bfloat16).reshape(TOKENS, C)
    joined = jnp.concatenate([hidden, epipolar], axis=1)
    merged = jnp.dot(joined, merge_weight, preferred_element_type=jnp.float32)
    activated = jax.nn.silu(group_norm(merged)).astype(jnp.bfloat16)
    projected = jnp.dot(activated, out_weight, preferred_element_type=jnp.float32)
    return (inputs + projected).astype(jnp.bfloat16)
```

```python
import jax
import jax.numpy as jnp
from jax import lax
from jax.sharding import PartitionSpec as P

GROUPS = 32
BLOCK = 128


def per_device(features, norm_gain, norm_shift, merge_weight, out_weight, corr_src, corr_count):
    devices = lax.axis_size("shard")
    rows_here, channels = features.shape
    blocks = rows_here // BLOCK
    slot_count = corr_src.shape[1]
    group_width = channels // GROUPS
    members = float(rows_here * group_width)
    slice_rows = BLOCK // devices
    all_blocks = corr_src.shape[0]

    def group_norm(values):
        grouped = values.reshape(rows_here, GROUPS, group_width)
        average = jnp.sum(grouped, axis=(0, 2), keepdims=True) / members
        centered = grouped - average
        variance = jnp.sum(centered * centered, axis=(0, 2), keepdims=True) / members
        return (centered * lax.rsqrt(variance + 1e-05)).reshape(rows_here, channels)

    inputs = features.astype(jnp.float32)
    hidden = jax.nn.silu(group_norm(inputs) * norm_gain + norm_shift).astype(jnp.bfloat16)
    slices = hidden.reshape(blocks, devices, slice_rows, channels).transpose(1, 0, 2, 3)
    arrived = lax.all_to_all(slices, "shard", split_axis=0, concat_axis=0, tiled=True)
    arrived = arrived.reshape(all_blocks, slice_rows, channels)
    valid = (jnp.arange(slot_count, dtype=jnp.int32)[None, :] < corr_count[:, None]).astype(jnp.float32)
    summed = jnp.zeros((all_blocks, slice_rows, channels), jnp.float32)
    for position in range(slot_count):
        picked = jnp.take(arrived, corr_src[:, position], axis=0, mode="clip")
        summed = summed + picked.astype(jnp.float32) * valid[:, position, None, None]
    divisor = corr_count.astype(jnp.float32)[:, None, None]
    pooled = (summed / divisor).astype(jnp.bfloat16).reshape(devices, blocks, slice_rows, channels)
    back = lax.all_to_all(pooled, "shard", split_axis=0, concat_axis=0, tiled=True)
    epipolar = back.transpose(1, 0, 2, 3).reshape(rows_here, channels)
    joined = jnp.concatenate([hidden, epipolar], axis=1)
    merged = jnp.dot(
        joined,
        lax.all_gather(merge_weight, "shard", axis=0, tiled=True),
        preferred_element_type=jnp.float32,
    )
    activated = jax.nn.silu(group_norm(merged)).astype(jnp.bfloat16)
    projected = jnp.dot(
        activated,
        lax.all_gather(out_weight, "shard", axis=0, tiled=True),
        preferred_element_type=jnp.float32,
    )
    return (inputs + projected).astype(jnp.bfloat16)


def solution(mesh):
    placed = (
        P(("grp", "shard"), None),
        P(),
        P(),
        P("shard", None),
        P("shard", None),
        P("grp", None),
        P("grp"),
    )
    return jax.shard_map(
        per_device, mesh=mesh, in_specs=placed, out_specs=P(("grp", "shard"), None), check_vma=False
    )
```

```python
import functools

import jax
import jax.numpy as jnp
from jax import lax
from jax.experimental import pallas as pl
from jax.experimental.pallas import tpu as pltpu
from jax.sharding import PartitionSpec as P

GROUPS = 32
BLOCK = 128
LANES = 128
ROWS = 8
PIECE = 16
MESH = pl.DeviceIdType.MESH
F32 = jnp.float32
BF16 = jnp.bfloat16


def zigzag(center, place):
    odd = place % 2
    return center + (1 - odd) * (place // 2) - odd * ((place + 1) // 2)


def split_rows(row):
    high = row.astype(BF16).astype(F32)
    rest = row - high
    middle = rest.astype(BF16).astype(F32)
    low = rest - middle
    fill = jnp.zeros((PIECE - 3, row.shape[1]), F32)
    return jnp.concatenate([high, middle, low, fill], axis=0).astype(BF16)


def group_mean(row, collect, spread, members):
    parts = jnp.dot(split_rows(row), collect[...], preferred_element_type=F32)
    mean = (parts[0:1] + parts[1:2] + parts[2:3]) / members
    parts = jnp.dot(split_rows(mean), spread[...], preferred_element_type=F32)
    return parts[0:1] + parts[1:2] + parts[2:3]


def fold_rows(values):
    return jnp.sum(values.reshape(values.shape[0] // ROWS, ROWS, values.shape[1]), axis=0)


def silu(values):
    return values / (1.0 + jnp.exp(-values))


def kernel(
    sizes,
    x_hbm, gain_ref, shift_ref, merge_ref, outw_ref, src_ref, count_ref,
    out_hbm,
    x, stage, send1, recv1, send2, recv2, table, full, merge_w, out_w, acc, collect, spread, stats,
    load_sem, out_sem, pack_sem, s1_sem, r1_sem, s2_sem, r2_sem, ws_sem, wr_sem,
):
    ys, zs, xs, cores = sizes
    shards = ys * zs
    rows, channels = x.shape
    blocks = rows // BLOCK
    strips = BLOCK // ROWS
    halves = shards // strips
    half = channels // halves
    chunks = half // LANES
    pieces = full.shape[1]
    merge_rows = merge_ref.shape[0]
    out_rows = outw_ref.shape[0]
    merge_pieces = merge_rows // PIECE
    group_width = channels // GROUPS
    members = float(rows * group_width)
    slice_rows = blocks * ROWS

    s = lax.axis_index("shard")
    g = lax.axis_index("grp")
    y, z = s // zs, s % zs
    xx, core = g // cores, g % cores

    load = pltpu.make_async_copy(x_hbm, x, load_sem)
    load.start()

    def peer_of(step):
        dz = zigzag(zs // 2, step // ys)
        dy = zigzag(ys // 2, step % ys)
        return ((y + dy) % ys) * zs + (z + dz) % zs

    barrier = pltpu.get_barrier_semaphore()

    @pl.loop(0, shards - 1)
    def _(step):
        pl.semaphore_signal(barrier, inc=1, device_id=(g, peer_of(step)), device_id_type=MESH)

    for dx in range(1, xs):
        to = ((xx + dx) % xs) * cores + core
        pl.semaphore_signal(barrier, inc=1, device_id=(to, s), device_id_type=MESH)
    sibling = xx * cores + (core + 1) % cores
    pl.semaphore_signal(barrier, inc=1, device_id=(sibling, s), device_id_type=MESH)

    for piece in range(merge_pieces):
        stage[piece] = merge_ref[piece * PIECE : (piece + 1) * PIECE, :]
    whole = out_rows // PIECE
    for piece in range(whole):
        stage[merge_pieces + piece] = outw_ref[piece * PIECE : (piece + 1) * PIECE, :]
    rest = out_rows - whole * PIECE
    tail = outw_ref[whole * PIECE : out_rows, :].astype(F32)
    stage[merge_pieces + whole] = jnp.concatenate(
        [tail, jnp.zeros((PIECE - rest, channels), F32)], axis=0
    ).astype(BF16)

    lane = lax.broadcasted_iota(jnp.int32, (channels, LANES), 1) * group_width
    row = lax.broadcasted_iota(jnp.int32, (channels, LANES), 0)
    collect[...] = jnp.where((row >= lane) & (row < lane + group_width), 1.0, 0.0).astype(BF16)
    lane = lax.broadcasted_iota(jnp.int32, (LANES, channels), 1)
    row = lax.broadcasted_iota(jnp.int32, (LANES, channels), 0) * group_width
    spread[...] = jnp.where((lane >= row) & (lane < row + group_width), 1.0, 0.0).astype(BF16)

    pl.semaphore_wait(barrier, shards - 1 + xs - 1 + 1)

    def weight_copy(source, target, stage_no, to):
        return pltpu.make_async_remote_copy(
            src_ref=source, dst_ref=target, send_sem=ws_sem.at[stage_no], recv_sem=wr_sem.at[stage_no],
            device_id=to, device_id_type=MESH,
        )

    def drain(ref, sem):
        pltpu.make_async_copy(ref, ref, sem).wait()

    pltpu.make_async_copy(stage.at[g], full.at[s, g], wr_sem.at[0]).start()
    for step in range(zs - 1):
        dz = zigzag(zs // 2, step)
        weight_copy(stage.at[g], full.at[s, g], 0, (g, y * zs + (z + dz) % zs)).start()

    load.wait()

    def total(i, carry):
        part = x[pl.ds(pl.multiple_of(i * 64, 64), 64), :].astype(F32)
        return carry + fold_rows(part)

    zeros = jnp.zeros((ROWS, channels), F32)
    summed = lax.fori_loop(0, rows // 64, total, zeros)
    average = group_mean(jnp.sum(summed, axis=0, keepdims=True), collect, spread, members)

    def total_square(i, carry):
        part = x[pl.ds(pl.multiple_of(i * 64, 64), 64), :].astype(F32) - average
        return carry + fold_rows(part * part)

    summed = lax.fori_loop(0, rows // 64, total_square, zeros)
    variance = group_mean(jnp.sum(summed, axis=0, keepdims=True), collect, spread, members)
    stats[0:1, :] = average
    stats[1:2, :] = lax.rsqrt(variance + 1e-05) * gain_ref[...]
    stats[2:3, :] = shift_ref[...]

    def exchange(source, target, chunk, send_sem, recv_sem):
        pltpu.make_async_copy(source.at[chunk, s], target.at[chunk, s], recv_sem.at[chunk]).start()

        @pl.loop(0, shards - 1)
        def _(step):
            to = peer_of(step)
            pltpu.make_async_remote_copy(
                src_ref=source.at[chunk, to], dst_ref=target.at[chunk, s],
                send_sem=send_sem.at[chunk], recv_sem=recv_sem.at[chunk],
                device_id=(g, to), device_id_type=MESH,
            ).start()

    @pl.loop(0, chunks)
    def _(chunk):
        @pl.loop(0, strips // 2)
        def _(pair):
            for side in range(halves):
                lanes = pl.ds(pl.multiple_of(side * half + chunk * LANES, LANES), LANES)
                average = stats[0:1, lanes]
                scale = stats[1:2, lanes]
                shift = stats[2:3, lanes]
                upper, lower = [], []
                for block in range(blocks):
                    at = pl.ds(pl.multiple_of(block * BLOCK + pair * 16, 16), 16)
                    value = silu((x[at, lanes].astype(F32) - average) * scale + shift)
                    upper.append(value[0:ROWS])
                    lower.append(value[ROWS : 2 * ROWS])
                send1[chunk, side * strips + 2 * pair] = jnp.concatenate(upper, axis=0).astype(BF16)
                send1[chunk, side * strips + 2 * pair + 1] = jnp.concatenate(lower, axis=0).astype(BF16)

        exchange(send1, recv1, chunk, s1_sem, r1_sem)

    drain(full.at[pl.ds(0, zs), 0], wr_sem.at[0])
    mine = full.at[pl.ds(y * zs, zs), g]
    for step in range(ys - 1):
        dy = zigzag(ys // 2, step)
        weight_copy(mine, mine, 1, (g, ((y + dy) % ys) * zs + z)).start()

    def gather(chunk):
        drain(recv1.at[chunk], r1_sem.at[chunk])

        @pl.loop(0, shards)
        def _(view):
            table[pl.ds(view * blocks, blocks)] = recv1[chunk, view].astype(F32).reshape(blocks, ROWS, LANES)

        @pl.loop(0, shards)
        def _(view):
            parts = []
            for block in range(blocks):
                k = view * blocks + block
                count = count_ref[k]
                second = jnp.where(count > 1, 1.0, 0.0).astype(F32)
                third = jnp.where(count > 2, 1.0, 0.0).astype(F32)
                share = jnp.where(count > 2, 1.0 / 3.0, jnp.where(count > 1, 0.5, 1.0)).astype(F32)
                value = table[src_ref[k, 0]] + table[src_ref[k, 1]] * second + table[src_ref[k, 2]] * third
                parts.append(value * share)
            send2[chunk, view] = jnp.concatenate(parts, axis=0).astype(BF16)

        exchange(send2, recv2, chunk, s2_sem, r2_sem)

    gather(0)

    drain(full.at[pl.ds(0, (ys - 1) * zs), 0], wr_sem.at[1])
    mine = full.at[:, g]
    for step in range(xs - 1):
        dx = zigzag(xs // 2, step)
        weight_copy(mine, mine, 2, (((xx + dx) % xs) * cores + core, s)).start()
    weight_copy(mine, mine, 3, (sibling, s)).start()

    @pl.loop(1, chunks)
    def _(chunk):
        gather(chunk)

    drain(full.at[pl.ds(0, (xs - 1) * shards // pieces)], wr_sem.at[2])
    for dx in range(1, xs):
        theirs = full.at[:, ((xx + dx) % xs) * cores + core]
        weight_copy(theirs, theirs, 3, (sibling, s)).start()
    drain(full.at[pl.ds(0, xs * shards // pieces)], wr_sem.at[3])

    @pl.loop(0, shards)
    def _(shard):
        for piece in range(merge_pieces):
            at = pl.ds(pl.multiple_of(shard * merge_rows + piece * PIECE, PIECE), PIECE)
            pltpu.make_async_copy(full.at[shard, piece], merge_w.at[at], pack_sem).start()

    @pl.loop(0, shards // 2)
    def _(pair):
        parts = []
        for member in range(2):
            for piece in range(whole + 1):
                part = full[2 * pair + member, merge_pieces + piece].astype(F32)
                parts.append(part if piece < whole else part[0:rest])
        at = pl.ds(pl.multiple_of(pair * 2 * out_rows, PIECE), 2 * out_rows)
        out_w[at, :] = jnp.concatenate(parts, axis=0).astype(BF16)

    drain(merge_w, pack_sem)

    tile = 256
    tile_strips = tile // slice_rows
    tiles = rows // tile

    def left(ref, chunk_list, side, m):
        at = pl.ds(side * strips + m * tile_strips, tile_strips)
        return jnp.concatenate([ref[chunk, at].reshape(tile, LANES) for chunk in chunk_list], axis=1)

    @pl.loop(0, tiles)
    def _(m):
        sides = [left(send1, range(chunks), side, m) for side in range(halves)]
        at = pl.ds(pl.multiple_of(m * tile, tile), tile)
        acc[at, :] = jnp.dot(
            jnp.concatenate(sides, axis=1), merge_w[0:channels, :], preferred_element_type=F32
        )

    def add_epipolar(chunk_list, m):
        depth = len(chunk_list) * LANES
        first = chunk_list[0] * LANES
        sides = [left(recv2, chunk_list, side, m) for side in range(halves)]
        weights = [
            merge_w[channels + side * half + first : channels + side * half + first + depth, :]
            for side in range(halves)
        ]
        at = pl.ds(pl.multiple_of(m * tile, tile), tile)
        value = acc[at, :] + jnp.dot(
            jnp.concatenate(sides, axis=1), jnp.concatenate(weights, axis=0), preferred_element_type=F32
        )
        acc[at, :] = value
        return value

    first = 0
    while first < chunks - 1:
        group = list(range(first, min(first + 2, chunks - 1)))
        for chunk in group:
            drain(recv2.at[chunk], r2_sem.at[chunk])

        @pl.loop(0, tiles)
        def _(m):
            add_epipolar(group, m)

        first += len(group)

    drain(recv2.at[chunks - 1], r2_sem.at[chunks - 1])

    def last(m, carry):
        return carry + fold_rows(add_epipolar([chunks - 1], m))

    summed = lax.fori_loop(0, tiles, last, zeros)
    average2 = group_mean(jnp.sum(summed, axis=0, keepdims=True), collect, spread, members)

    def last_square(i, carry):
        part = acc[pl.ds(pl.multiple_of(i * 64, 64), 64), :] - average2
        return carry + fold_rows(part * part)

    summed = lax.fori_loop(0, rows // 64, last_square, zeros)
    variance2 = group_mean(jnp.sum(summed, axis=0, keepdims=True), collect, spread, members)
    stats[0:1, :] = average2
    stats[1:2, :] = lax.rsqrt(variance2 + 1e-05)

    @pl.loop(0, tiles)
    def _(m):
        at = pl.ds(pl.multiple_of(m * tile, tile), tile)
        value = silu((acc[at, :] - stats[0:1, :]) * stats[1:2, :]).astype(BF16)
        projected = jnp.dot(value, out_w[...], preferred_element_type=F32)
        for pair in range(tile_strips // 2):
            top = 2 * pair * slice_rows
            for block in range(blocks):
                both = jnp.concatenate(
                    [
                        projected[top + block * ROWS : top + (block + 1) * ROWS],
                        projected[top + slice_rows + block * ROWS : top + slice_rows + (block + 1) * ROWS],
                    ],
                    axis=0,
                )
                to = pl.ds(
                    pl.multiple_of(block * BLOCK + m * (tile_strips * ROWS) + pair * 16, 16), 16
                )
                x[to, :] = (x[to, :].astype(F32) + both).astype(BF16)
        for block in range(blocks):
            to = pl.ds(
                pl.multiple_of(block * BLOCK + m * (tile_strips * ROWS), tile_strips * ROWS), tile_strips * ROWS
            )
            pltpu.make_async_copy(x.at[to], out_hbm.at[to], out_sem).start()

    for chunk in range(chunks):
        drain(send1.at[chunk, pl.ds(0, shards - 1)], s1_sem.at[chunk])
        drain(send2.at[chunk, pl.ds(0, shards - 1)], s2_sem.at[chunk])
    drain(full.at[pl.ds(0, zs - 1), 0], ws_sem.at[0])
    drain(full.at[pl.ds(0, (ys - 1) * zs), 0], ws_sem.at[1])
    drain(full.at[pl.ds(0, (xs - 1) * shards // pieces)], ws_sem.at[2])
    drain(full.at[pl.ds(0, xs * shards // pieces)], ws_sem.at[3])
    drain(x, out_sem)


def solution(mesh):
    sizes = (4, 8, 4, 2)

    def per_device(features, norm_gain, norm_shift, merge_weight, out_weight, corr_src, corr_count):
        rows, channels = features.shape
        shards = lax.axis_size("shard")
        groups = lax.axis_size("grp")
        slice_rows = rows // BLOCK * ROWS
        chunks = channels // (shards // (BLOCK // ROWS)) // LANES
        vmem = pl.BlockSpec(memory_space=pltpu.VMEM)
        smem = pl.BlockSpec(memory_space=pltpu.SMEM)
        hbm = pl.BlockSpec(memory_space=pl.ANY)
        slices = pltpu.VMEM((chunks, shards, slice_rows, LANES), BF16)
        dma = pltpu.SemaphoreType.DMA
        return pl.pallas_call(
            functools.partial(kernel, sizes),
            out_shape=jax.ShapeDtypeStruct(features.shape, features.dtype),
            in_specs=[hbm, vmem, vmem, vmem, vmem, smem, smem],
            out_specs=hbm,
            scratch_shapes=[
                pltpu.VMEM((rows, channels), BF16),
                pltpu.VMEM((groups, PIECE, channels), BF16),
                slices, slices, slices, slices,
                pltpu.VMEM((corr_src.shape[0], ROWS, LANES), F32),
                pltpu.VMEM((shards, groups, PIECE, channels), BF16),
                pltpu.VMEM((2 * channels, channels), BF16),
                pltpu.VMEM((channels, channels), BF16),
                pltpu.VMEM((rows, channels), F32),
                pltpu.VMEM((channels, LANES), BF16),
                pltpu.VMEM((LANES, channels), BF16),
                pltpu.VMEM((ROWS, channels), F32),
                dma, dma, dma,
                dma((chunks,)), dma((chunks,)), dma((chunks,)), dma((chunks,)),
                dma((4,)), dma((4,)),
            ],
            compiler_params=pltpu.CompilerParams(
                collective_id=0, has_side_effects=True, vmem_limit_bytes=60 * 1024 * 1024
            ),
            name="merge_block",
        )(
            features, norm_gain.reshape(1, channels), norm_shift.reshape(1, channels),
            merge_weight, out_weight, corr_src, corr_count,
        )

    placed = (
        P(("grp", "shard"), None),
        P(),
        P(),
        P("shard", None),
        P("shard", None),
        P("grp", None),
        P("grp"),
    )
    return jax.shard_map(
        per_device, mesh=mesh, in_specs=placed, out_specs=P(("grp", "shard"), None), check_vma=False
    )
```

```python
import functools

import jax
import jax.numpy as jnp
from jax import lax
from jax.experimental import pallas as pl
from jax.experimental.pallas import tpu as pltpu
from jax.sharding import PartitionSpec as P

GROUPS = 32
BLOCK = 128
LANES = 128
ROWS = 8
PIECE = 16
MESH = pl.DeviceIdType.MESH
F32 = jnp.float32
BF16 = jnp.bfloat16


def zigzag(center, place):
    odd = place % 2
    return center + (1 - odd) * (place // 2) - odd * ((place + 1) // 2)


def split_rows(row):
    high = row.astype(BF16).astype(F32)
    rest = row - high
    middle = rest.astype(BF16).astype(F32)
    low = rest - middle
    fill = jnp.zeros((PIECE - 3, row.shape[1]), F32)
    return jnp.concatenate([high, middle, low, fill], axis=0).astype(BF16)


def group_mean(row, collect, spread, members):
    parts = jnp.dot(split_rows(row), collect[...], preferred_element_type=F32)
    mean = (parts[0:1] + parts[1:2] + parts[2:3]) / members
    parts = jnp.dot(split_rows(mean), spread[...], preferred_element_type=F32)
    return parts[0:1] + parts[1:2] + parts[2:3]


def fold_rows(values):
    return jnp.sum(values.reshape(values.shape[0] // ROWS, ROWS, values.shape[1]), axis=0)


def silu(values):
    middle = 0.5 * values
    return middle + middle * jnp.tanh(middle)


def kernel(
    sizes,
    x_hbm, gain_hbm, shift_hbm, merge_hbm, outw_hbm, src_hbm, count_hbm,
    out_hbm,
    x, params, merge_ref, outw_ref, src_ref, count_ref, stage, send1, recv1, send2, recv2, table, full, merge_w, out_w, acc, collect, spread, stats,
    load_sem, out_sem, pack_sem, s1_sem, r1_sem, s2_sem, r2_sem, ws_sem, wr_sem,
):
    ys, zs, xs, cores = sizes
    shards = ys * zs
    rows, channels = x.shape
    blocks = rows // BLOCK
    strips = BLOCK // ROWS
    halves = shards // strips
    half = channels // halves
    chunks = half // LANES
    pieces = full.shape[1]
    merge_rows = merge_ref.shape[0]
    out_rows = outw_ref.shape[0]
    merge_pieces = merge_rows // PIECE
    group_width = channels // GROUPS
    members = float(rows * group_width)
    slice_rows = blocks * ROWS

    s = lax.axis_index("shard")
    g = lax.axis_index("grp")
    y, z = s // zs, s % zs
    xx, core = g // cores, g % cores

    load = pltpu.make_async_copy(x_hbm, x, load_sem.at[0])
    load.start()
    fetches = [
        pltpu.make_async_copy(source, target, load_sem.at[1 + i])
        for i, (source, target) in enumerate(
            (
                (merge_hbm, merge_ref), (outw_hbm, outw_ref), (gain_hbm, params.at[0]), (shift_hbm, params.at[1]),
                (src_hbm, src_ref), (count_hbm, count_ref),
            )
        )
    ]
    for fetch in fetches:
        fetch.start()

    def peer_of(step):
        dz = zigzag(zs // 2, step // ys)
        dy = zigzag(ys // 2, step % ys)
        return ((y + dy) % ys) * zs + (z + dz) % zs

    barrier = pltpu.get_barrier_semaphore()

    @pl.loop(0, shards - 1)
    def _(step):
        pl.semaphore_signal(barrier, inc=1, device_id=(g, peer_of(step)), device_id_type=MESH)

    for dx in range(1, xs):
        to = ((xx + dx) % xs) * cores + core
        pl.semaphore_signal(barrier, inc=1, device_id=(to, s), device_id_type=MESH)
    sibling = xx * cores + (core + 1) % cores
    pl.semaphore_signal(barrier, inc=1, device_id=(sibling, s), device_id_type=MESH)

    lane = lax.broadcasted_iota(jnp.int32, (channels, LANES), 1) * group_width
    row = lax.broadcasted_iota(jnp.int32, (channels, LANES), 0)
    collect[...] = jnp.where((row >= lane) & (row < lane + group_width), 1.0, 0.0).astype(BF16)
    lane = lax.broadcasted_iota(jnp.int32, (LANES, channels), 1)
    row = lax.broadcasted_iota(jnp.int32, (LANES, channels), 0) * group_width
    spread[...] = jnp.where((lane >= row) & (lane < row + group_width), 1.0, 0.0).astype(BF16)

    def weight_copy(source, target, stage_no, to):
        return pltpu.make_async_remote_copy(
            src_ref=source, dst_ref=target, send_sem=ws_sem.at[stage_no], recv_sem=wr_sem.at[stage_no],
            device_id=to, device_id_type=MESH,
        )

    def drain(ref, sem):
        pltpu.make_async_copy(ref, ref, sem).wait()

    load.wait()

    def total(i, carry):
        part = x[pl.ds(pl.multiple_of(i * 64, 64), 64), :].astype(F32)
        return carry + fold_rows(part)

    zeros = jnp.zeros((ROWS, channels), F32)
    summed = lax.fori_loop(0, rows // 64, total, zeros)
    average = group_mean(jnp.sum(summed, axis=0, keepdims=True), collect, spread, members)

    def total_square(i, carry):
        part = x[pl.ds(pl.multiple_of(i * 64, 64), 64), :].astype(F32) - average
        return carry + fold_rows(part * part)

    summed = lax.fori_loop(0, rows // 64, total_square, zeros)
    variance = group_mean(jnp.sum(summed, axis=0, keepdims=True), collect, spread, members)
    stats[0:1, :] = average
    fetches[2].wait()
    fetches[3].wait()
    stats[1:2, :] = lax.rsqrt(variance + 1e-05) * params[0:1, :]
    stats[2:3, :] = params[1:2, :]

    def exchange(source, target, chunk, send_sem, recv_sem):
        pltpu.make_async_copy(source.at[chunk, s], target.at[chunk, s], recv_sem.at[chunk]).start()

        @pl.loop(0, shards - 1)
        def _(step):
            to = peer_of(step)
            pltpu.make_async_remote_copy(
                src_ref=source.at[chunk, to], dst_ref=target.at[chunk, s],
                send_sem=send_sem.at[chunk], recv_sem=recv_sem.at[chunk],
                device_id=(g, to), device_id_type=MESH,
            ).start()

    def hide(chunk):
        @pl.loop(0, strips // 2)
        def _(pair):
            for side in range(halves):
                lanes = pl.ds(pl.multiple_of(side * half + chunk * LANES, LANES), LANES)
                average = stats[0:1, lanes]
                scale = stats[1:2, lanes]
                shift = stats[2:3, lanes]
                upper, lower = [], []
                for block in range(blocks):
                    at = pl.ds(pl.multiple_of(block * BLOCK + pair * 16, 16), 16)
                    value = silu((x[at, lanes].astype(F32) - average) * scale + shift)
                    upper.append(value[0:ROWS])
                    lower.append(value[ROWS : 2 * ROWS])
                send1[chunk, side * strips + 2 * pair] = jnp.concatenate(upper, axis=0).astype(BF16)
                send1[chunk, side * strips + 2 * pair + 1] = jnp.concatenate(lower, axis=0).astype(BF16)

    fetches[0].wait()
    fetches[1].wait()

    for piece in range(merge_pieces):
        stage[piece] = merge_ref[piece * PIECE : (piece + 1) * PIECE, :]
    whole = out_rows // PIECE
    for piece in range(whole):
        stage[merge_pieces + piece] = outw_ref[piece * PIECE : (piece + 1) * PIECE, :]
    rest = out_rows - whole * PIECE
    tail = outw_ref[whole * PIECE : out_rows, :].astype(F32)
    stage[merge_pieces + whole] = jnp.concatenate(
        [tail, jnp.zeros((PIECE - rest, channels), F32)], axis=0
    ).astype(BF16)

    hide(0)
    pl.semaphore_wait(barrier, shards - 1 + xs - 1 + 1)

    pltpu.make_async_copy(stage.at[g], full.at[s, g], wr_sem.at[0]).start()
    for step in range(zs - 1):
        dz = zigzag(zs // 2, step)
        weight_copy(stage.at[g], full.at[s, g], 0, (g, y * zs + (z + dz) % zs)).start()

    exchange(send1, recv1, 0, s1_sem, r1_sem)

    @pl.loop(1, chunks)
    def _(chunk):
        hide(chunk)
        exchange(send1, recv1, chunk, s1_sem, r1_sem)

    drain(full.at[pl.ds(0, zs), 0], wr_sem.at[0])
    mine = full.at[pl.ds(y * zs, zs), g]
    for step in range(ys - 1):
        dy = zigzag(ys // 2, step)
        weight_copy(mine, mine, 1, (g, ((y + dy) % ys) * zs + z)).start()

    def gather(chunk):
        drain(recv1.at[chunk], r1_sem.at[chunk])

        @pl.loop(0, shards)
        def _(view):
            table[pl.ds(view * blocks, blocks)] = recv1[chunk, view].astype(F32).reshape(blocks, ROWS, LANES)

        @pl.loop(0, shards)
        def _(view):
            parts = []
            for block in range(blocks):
                k = view * blocks + block
                count = count_ref[k]
                second = jnp.where(count > 1, 1.0, 0.0).astype(F32)
                third = jnp.where(count > 2, 1.0, 0.0).astype(F32)
                share = jnp.where(count > 2, 1.0 / 3.0, jnp.where(count > 1, 0.5, 1.0)).astype(F32)
                value = table[src_ref[0, k]] + table[src_ref[1, k]] * second + table[src_ref[2, k]] * third
                parts.append(value * share)
            send2[chunk, view] = jnp.concatenate(parts, axis=0).astype(BF16)

        exchange(send2, recv2, chunk, s2_sem, r2_sem)

    fetches[4].wait()
    fetches[5].wait()
    gather(0)

    drain(full.at[pl.ds(0, (ys - 1) * zs), 0], wr_sem.at[1])
    mine = full.at[:, g]
    for step in range(xs - 1):
        dx = zigzag(xs // 2, step)
        weight_copy(mine, mine, 2, (((xx + dx) % xs) * cores + core, s)).start()
    weight_copy(mine, mine, 3, (sibling, s)).start()

    @pl.loop(1, chunks)
    def _(chunk):
        gather(chunk)

    drain(full.at[pl.ds(0, (xs - 1) * shards // pieces)], wr_sem.at[2])
    for dx in range(1, xs):
        theirs = full.at[:, ((xx + dx) % xs) * cores + core]
        weight_copy(theirs, theirs, 3, (sibling, s)).start()
    drain(full.at[pl.ds(0, xs * shards // pieces)], wr_sem.at[3])

    @pl.loop(0, shards)
    def _(shard):
        for piece in range(merge_pieces):
            at = pl.ds(pl.multiple_of(shard * merge_rows + piece * PIECE, PIECE), PIECE)
            pltpu.make_async_copy(full.at[shard, piece], merge_w.at[at], pack_sem).start()

    @pl.loop(0, shards // 2)
    def _(pair):
        parts = []
        for member in range(2):
            for piece in range(whole + 1):
                part = full[2 * pair + member, merge_pieces + piece].astype(F32)
                parts.append(part if piece < whole else part[0:rest])
        at = pl.ds(pl.multiple_of(pair * 2 * out_rows, PIECE), 2 * out_rows)
        out_w[at, :] = jnp.concatenate(parts, axis=0).astype(BF16)

    drain(merge_w, pack_sem)

    tile = 256
    tile_strips = tile // slice_rows
    tiles = rows // tile

    def left(ref, chunk_list, side, m):
        at = pl.ds(side * strips + m * tile_strips, tile_strips)
        return jnp.concatenate([ref[chunk, at].reshape(tile, LANES) for chunk in chunk_list], axis=1)

    @pl.loop(0, tiles)
    def _(m):
        sides = [left(send1, range(chunks), side, m) for side in range(halves)]
        at = pl.ds(pl.multiple_of(m * tile, tile), tile)
        acc[at, :] = jnp.dot(
            jnp.concatenate(sides, axis=1), merge_w[0:channels, :], preferred_element_type=F32
        )

    def add_epipolar(chunk_list, m):
        depth = len(chunk_list) * LANES
        first = chunk_list[0] * LANES
        sides = [left(recv2, chunk_list, side, m) for side in range(halves)]
        weights = [
            merge_w[channels + side * half + first : channels + side * half + first + depth, :]
            for side in range(halves)
        ]
        at = pl.ds(pl.multiple_of(m * tile, tile), tile)
        value = acc[at, :] + jnp.dot(
            jnp.concatenate(sides, axis=1), jnp.concatenate(weights, axis=0), preferred_element_type=F32
        )
        acc[at, :] = value
        return value

    first = 0
    while first < chunks - 1:
        group = list(range(first, min(first + 2, chunks - 1)))
        for chunk in group:
            drain(recv2.at[chunk], r2_sem.at[chunk])

        @pl.loop(0, tiles)
        def _(m):
            add_epipolar(group, m)

        first += len(group)

    def partial(i, carry):
        return carry + fold_rows(acc[pl.ds(pl.multiple_of(i * 64, 64), 64), :])

    summed = lax.fori_loop(0, rows // 64, partial, zeros)
    stats[0:1, :] = group_mean(jnp.sum(summed, axis=0, keepdims=True), collect, spread, members)

    drain(recv2.at[chunks - 1], r2_sem.at[chunks - 1])

    def last(m, carry):
        difference = add_epipolar([chunks - 1], m) - stats[0:1, :]
        return carry[0] + fold_rows(difference), carry[1] + fold_rows(difference * difference)

    summed, squares = lax.fori_loop(0, tiles, last, (zeros, zeros))
    moved = group_mean(jnp.sum(summed, axis=0, keepdims=True), collect, spread, members)
    square = group_mean(jnp.sum(squares, axis=0, keepdims=True), collect, spread, members)
    stats[0:1, :] = stats[0:1, :] + moved
    stats[1:2, :] = lax.rsqrt(jnp.maximum(square - moved * moved, 0.0) + 1e-05)

    @pl.loop(0, tiles)
    def _(m):
        at = pl.ds(pl.multiple_of(m * tile, tile), tile)
        value = silu((acc[at, :] - stats[0:1, :]) * stats[1:2, :]).astype(BF16)
        projected = jnp.dot(value, out_w[...], preferred_element_type=F32)
        for pair in range(tile_strips // 2):
            top = 2 * pair * slice_rows
            for block in range(blocks):
                both = jnp.concatenate(
                    [
                        projected[top + block * ROWS : top + (block + 1) * ROWS],
                        projected[top + slice_rows + block * ROWS : top + slice_rows + (block + 1) * ROWS],
                    ],
                    axis=0,
                )
                to = pl.ds(
                    pl.multiple_of(block * BLOCK + m * (tile_strips * ROWS) + pair * 16, 16), 16
                )
                x[to, :] = (x[to, :].astype(F32) + both).astype(BF16)
        for block in range(blocks):
            to = pl.ds(
                pl.multiple_of(block * BLOCK + m * (tile_strips * ROWS), tile_strips * ROWS), tile_strips * ROWS
            )
            pltpu.make_async_copy(x.at[to], out_hbm.at[to], out_sem).start()

    for chunk in range(chunks):
        drain(send1.at[chunk, pl.ds(0, shards - 1)], s1_sem.at[chunk])
        drain(send2.at[chunk, pl.ds(0, shards - 1)], s2_sem.at[chunk])
    drain(full.at[pl.ds(0, zs - 1), 0], ws_sem.at[0])
    drain(full.at[pl.ds(0, (ys - 1) * zs), 0], ws_sem.at[1])
    drain(full.at[pl.ds(0, (xs - 1) * shards // pieces)], ws_sem.at[2])
    drain(full.at[pl.ds(0, xs * shards // pieces)], ws_sem.at[3])
    drain(x, out_sem)


def solution(mesh):
    sizes = (4, 8, 4, 2)

    def per_device(features, norm_gain, norm_shift, merge_weight, out_weight, corr_src, corr_count):
        rows, channels = features.shape
        shards = lax.axis_size("shard")
        groups = lax.axis_size("grp")
        slice_rows = rows // BLOCK * ROWS
        chunks = channels // (shards // (BLOCK // ROWS)) // LANES
        hbm = pl.BlockSpec(memory_space=pltpu.HBM)
        slices = pltpu.VMEM((chunks, shards, slice_rows, LANES), BF16)
        dma = pltpu.SemaphoreType.DMA
        return pl.pallas_call(
            functools.partial(kernel, sizes),
            out_shape=jax.ShapeDtypeStruct(features.shape, features.dtype),
            in_specs=[hbm] * 7,
            out_specs=pl.BlockSpec(memory_space=pl.ANY),
            scratch_shapes=[
                pltpu.VMEM((rows, channels), BF16),
                pltpu.VMEM((ROWS, channels), F32),
                pltpu.VMEM(merge_weight.shape, BF16),
                pltpu.VMEM(out_weight.shape, BF16),
                pltpu.SMEM(corr_src.shape[::-1], jnp.int32),
                pltpu.SMEM(corr_count.shape, jnp.int32),
                pltpu.VMEM((groups, PIECE, channels), BF16),
                slices, slices, slices, slices,
                pltpu.VMEM((corr_src.shape[0], ROWS, LANES), F32),
                pltpu.VMEM((shards, groups, PIECE, channels), BF16),
                pltpu.VMEM((2 * channels, channels), BF16),
                pltpu.VMEM((channels, channels), BF16),
                pltpu.VMEM((rows, channels), F32),
                pltpu.VMEM((channels, LANES), BF16),
                pltpu.VMEM((LANES, channels), BF16),
                pltpu.VMEM((ROWS, channels), F32),
                dma((7,)), dma, dma,
                dma((chunks,)), dma((chunks,)), dma((chunks,)), dma((chunks,)),
                dma((4,)), dma((4,)),
            ],
            compiler_params=pltpu.CompilerParams(
                collective_id=0, has_side_effects=True, vmem_limit_bytes=44 * 1024 * 1024
            ),
            name="merge_block",
        )(
            *(
                pltpu.with_memory_space_constraint(array, pltpu.HBM)
                for array in (
                    features, norm_gain, norm_shift, merge_weight, out_weight, corr_src.T, corr_count
                )
            )
        )

    placed = (
        P(("grp", "shard"), None),
        P(),
        P(),
        P("shard", None),
        P("shard", None),
        P("grp", None),
        P("grp"),
    )
    return jax.shard_map(
        per_device, mesh=mesh, in_specs=placed, out_specs=P(("grp", "shard"), None), check_vma=False
    )
```

```python
import functools

import jax
import jax.numpy as jnp
from jax import lax
from jax.experimental import pallas as pl
from jax.experimental.pallas import tpu as pltpu
from jax.sharding import PartitionSpec as P

GROUPS = 32
BLOCK = 128
LANES = 128
ROWS = 8
PIECE = 16
MESH = pl.DeviceIdType.MESH
F32 = jnp.float32
BF16 = jnp.bfloat16


def zigzag(center, place):
    odd = place % 2
    return center + (1 - odd) * (place // 2) - odd * ((place + 1) // 2)


def exact_rows(rows, matrix):
    parts = []
    for row in rows:
        high = row.astype(BF16).astype(F32)
        rest = row - high
        middle = rest.astype(BF16).astype(F32)
        parts += [high, middle, rest - middle]
    parts.append(jnp.zeros((PIECE - len(parts), rows[0].shape[1]), F32))
    stacked = jnp.concatenate(parts, axis=0).astype(BF16)
    product = jnp.dot(stacked, matrix[...], preferred_element_type=F32)
    return [product[i : i + 1] + product[i + 1 : i + 2] + product[i + 2 : i + 3] for i in range(0, 3 * len(rows), 3)]


def group_mean(row, collect, spread, members):
    (total,) = exact_rows([row], collect)
    return exact_rows([total / members], spread)[0]


def fold_rows(values):
    return jnp.sum(values.reshape(values.shape[0] // ROWS, ROWS, values.shape[1]), axis=0)


def silu(values):
    middle = 0.5 * values
    return middle + middle * jnp.tanh(middle)


def kernel(
    sizes,
    x_hbm, gain_hbm, shift_hbm, merge_hbm, outw_hbm, src_hbm, count_hbm,
    out_ref,
    x, params, merge_ref, outw_ref, src_ref, count_ref, stage, send1, recv1, send2, recv2, table, full, merge_w, out_w, acc, act, collect, spread, stats,
    load_sem, s1_sem, r1_sem, s2_sem, r2_sem, ws_sem, wr_sem,
):
    ys, zs, xs, cores = sizes
    shards = ys * zs
    rows, channels = x.shape
    blocks = rows // BLOCK
    strips = BLOCK // ROWS
    halves = shards // strips
    half = channels // halves
    chunks = half // LANES
    pieces = full.shape[1]
    merge_rows = merge_ref.shape[0]
    out_rows = outw_ref.shape[0]
    merge_pieces = merge_rows // PIECE
    group_width = channels // GROUPS
    members = float(rows * group_width)
    slice_rows = blocks * ROWS

    s = lax.axis_index("shard")
    g = lax.axis_index("grp")
    y, z = s // zs, s % zs
    xx, core = g // cores, g % cores

    load = pltpu.make_async_copy(x_hbm, x, load_sem.at[0])
    load.start()
    fetches = [
        pltpu.make_async_copy(source, target, load_sem.at[1 + i])
        for i, (source, target) in enumerate(
            (
                (merge_hbm, merge_ref), (outw_hbm, outw_ref), (gain_hbm, params.at[0]), (shift_hbm, params.at[1]),
                (src_hbm, src_ref), (count_hbm, count_ref),
            )
        )
    ]
    for fetch in fetches:
        fetch.start()

    def peer_of(step):
        dz = zigzag(zs // 2, step // ys)
        dy = zigzag(ys // 2, step % ys)
        return ((y + dy) % ys) * zs + (z + dz) % zs

    barrier = pltpu.get_barrier_semaphore()

    @pl.loop(0, shards - 1)
    def _(step):
        pl.semaphore_signal(barrier, inc=1, device_id=(g, peer_of(step)), device_id_type=MESH)

    for dx in range(1, xs):
        to = ((xx + dx) % xs) * cores + core
        pl.semaphore_signal(barrier, inc=1, device_id=(to, s), device_id_type=MESH)
    sibling = xx * cores + (core + 1) % cores
    pl.semaphore_signal(barrier, inc=1, device_id=(sibling, s), device_id_type=MESH)

    lane = lax.broadcasted_iota(jnp.int32, (channels, LANES), 1) * group_width
    row = lax.broadcasted_iota(jnp.int32, (channels, LANES), 0)
    collect[...] = jnp.where((row >= lane) & (row < lane + group_width), 1.0, 0.0).astype(BF16)
    lane = lax.broadcasted_iota(jnp.int32, (LANES, channels), 1)
    row = lax.broadcasted_iota(jnp.int32, (LANES, channels), 0) * group_width
    spread[...] = jnp.where((lane >= row) & (lane < row + group_width), 1.0, 0.0).astype(BF16)

    def weight_copy(source, target, stage_no, to):
        return pltpu.make_async_remote_copy(
            src_ref=source, dst_ref=target, send_sem=ws_sem.at[stage_no], recv_sem=wr_sem.at[stage_no],
            device_id=to, device_id_type=MESH,
        )

    def drain(ref, sem):
        pltpu.make_async_copy(ref, ref, sem).wait()

    load.wait()

    def total(i, carry):
        part = x[pl.ds(pl.multiple_of(i * 64, 64), 64), :].astype(F32)
        return carry + fold_rows(part)

    zeros = jnp.zeros((ROWS, channels), F32)
    summed = lax.fori_loop(0, rows // 64, total, zeros)
    average = group_mean(jnp.sum(summed, axis=0, keepdims=True), collect, spread, members)

    def total_square(i, carry):
        part = x[pl.ds(pl.multiple_of(i * 64, 64), 64), :].astype(F32) - average
        return carry + fold_rows(part * part)

    summed = lax.fori_loop(0, rows // 64, total_square, zeros)
    variance = group_mean(jnp.sum(summed, axis=0, keepdims=True), collect, spread, members)
    stats[0:1, :] = average
    fetches[2].wait()
    fetches[3].wait()
    stats[1:2, :] = lax.rsqrt(variance + 1e-05) * params[0:1, :]
    stats[2:3, :] = params[1:2, :]

    def exchange(source, target, chunk, send_sem, recv_sem):
        pltpu.make_async_copy(source.at[chunk, s], target.at[chunk, s], recv_sem.at[chunk]).start()

        @pl.loop(0, shards - 1)
        def _(step):
            to = peer_of(step)
            pltpu.make_async_remote_copy(
                src_ref=source.at[chunk, to], dst_ref=target.at[chunk, s],
                send_sem=send_sem.at[chunk], recv_sem=recv_sem.at[chunk],
                device_id=(g, to), device_id_type=MESH,
            ).start()

    def hide(chunk):
        @pl.loop(0, strips // 2)
        def _(pair):
            for side in range(halves):
                lanes = pl.ds(pl.multiple_of(side * half + chunk * LANES, LANES), LANES)
                average = stats[0:1, lanes]
                scale = stats[1:2, lanes]
                shift = stats[2:3, lanes]
                upper, lower = [], []
                for block in range(blocks):
                    at = pl.ds(pl.multiple_of(block * BLOCK + pair * 16, 16), 16)
                    value = silu((x[at, lanes].astype(F32) - average) * scale + shift)
                    upper.append(value[0:ROWS])
                    lower.append(value[ROWS : 2 * ROWS])
                send1[chunk, side * strips + 2 * pair] = jnp.concatenate(upper, axis=0).astype(BF16)
                send1[chunk, side * strips + 2 * pair + 1] = jnp.concatenate(lower, axis=0).astype(BF16)

    fetches[0].wait()
    fetches[1].wait()

    for piece in range(merge_pieces):
        stage[piece] = merge_ref[piece * PIECE : (piece + 1) * PIECE, :]
    whole = out_rows // PIECE
    for piece in range(whole):
        stage[merge_pieces + piece] = outw_ref[piece * PIECE : (piece + 1) * PIECE, :]
    rest = out_rows - whole * PIECE
    tail = outw_ref[whole * PIECE : out_rows, :].astype(F32)
    stage[merge_pieces + whole] = jnp.concatenate(
        [tail, jnp.zeros((PIECE - rest, channels), F32)], axis=0
    ).astype(BF16)

    hide(0)
    pl.semaphore_wait(barrier, shards - 1 + xs - 1 + 1)

    pltpu.make_async_copy(stage.at[g], full.at[s, g], wr_sem.at[0]).start()
    for step in range(zs - 1):
        dz = zigzag(zs // 2, step)
        weight_copy(stage.at[g], full.at[s, g], 0, (g, y * zs + (z + dz) % zs)).start()

    exchange(send1, recv1, 0, s1_sem, r1_sem)

    @pl.loop(1, chunks)
    def _(chunk):
        hide(chunk)
        exchange(send1, recv1, chunk, s1_sem, r1_sem)

    drain(full.at[pl.ds(0, zs), 0], wr_sem.at[0])
    mine = full.at[pl.ds(y * zs, zs), g]
    for step in range(ys - 1):
        dy = zigzag(ys // 2, step)
        weight_copy(mine, mine, 1, (g, ((y + dy) % ys) * zs + z)).start()

    def gather(chunk):
        drain(recv1.at[chunk], r1_sem.at[chunk])

        @pl.loop(0, shards)
        def _(view):
            table[pl.ds(view * blocks, blocks)] = recv1[chunk, view].astype(F32).reshape(blocks, ROWS, LANES)

        @pl.loop(0, shards)
        def _(view):
            parts = []
            for block in range(blocks):
                k = view * blocks + block
                count = count_ref[k]
                second = jnp.where(count > 1, 1.0, 0.0).astype(F32)
                third = jnp.where(count > 2, 1.0, 0.0).astype(F32)
                share = jnp.where(count > 2, 1.0 / 3.0, jnp.where(count > 1, 0.5, 1.0)).astype(F32)
                value = table[src_ref[0, k]] + table[src_ref[1, k]] * second + table[src_ref[2, k]] * third
                parts.append(value * share)
            send2[chunk, view] = jnp.concatenate(parts, axis=0).astype(BF16)

        exchange(send2, recv2, chunk, s2_sem, r2_sem)

    fetches[4].wait()
    fetches[5].wait()
    gather(0)

    drain(full.at[pl.ds(0, (ys - 1) * zs), 0], wr_sem.at[1])
    mine = full.at[:, g]
    for step in range(xs - 1):
        dx = zigzag(xs // 2, step)
        weight_copy(mine, mine, 2, (((xx + dx) % xs) * cores + core, s)).start()
    weight_copy(mine, mine, 3, (sibling, s)).start()

    @pl.loop(1, chunks)
    def _(chunk):
        gather(chunk)

    drain(full.at[pl.ds(0, (xs - 1) * shards // pieces)], wr_sem.at[2])
    for dx in range(1, xs):
        theirs = full.at[:, ((xx + dx) % xs) * cores + core]
        weight_copy(theirs, theirs, 3, (sibling, s)).start()
    drain(full.at[pl.ds(0, xs * shards // pieces)], wr_sem.at[3])

    @pl.loop(0, shards)
    def _(shard):
        for piece in range(merge_pieces):
            at = pl.ds(pl.multiple_of(shard * merge_rows + piece * PIECE, PIECE), PIECE)
            merge_w[at, :] = full[shard, piece]

    @pl.loop(0, shards // 2)
    def _(pair):
        parts = []
        for member in range(2):
            for piece in range(whole + 1):
                part = full[2 * pair + member, merge_pieces + piece].astype(F32)
                parts.append(part if piece < whole else part[0:rest])
        at = pl.ds(pl.multiple_of(pair * 2 * out_rows, PIECE), 2 * out_rows)
        out_w[at, :] = jnp.concatenate(parts, axis=0).astype(BF16)

    tile = 256
    tile_strips = tile // slice_rows
    tiles = rows // tile

    def left(ref, chunk_list, side, m):
        at = pl.ds(side * strips + m * tile_strips, tile_strips)
        return jnp.concatenate([ref[chunk, at].reshape(tile, LANES) for chunk in chunk_list], axis=1)

    @pl.loop(0, tiles)
    def _(m):
        sides = [left(send1, range(chunks), side, m) for side in range(halves)]
        at = pl.ds(pl.multiple_of(m * tile, tile), tile)
        acc[at, :] = jnp.dot(
            jnp.concatenate(sides, axis=1), merge_w[0:channels, :], preferred_element_type=F32
        )

    def add_epipolar(chunk_list, m):
        depth = len(chunk_list) * LANES
        first = chunk_list[0] * LANES
        sides = [left(recv2, chunk_list, side, m) for side in range(halves)]
        weights = [
            merge_w[channels + side * half + first : channels + side * half + first + depth, :]
            for side in range(halves)
        ]
        at = pl.ds(pl.multiple_of(m * tile, tile), tile)
        value = acc[at, :] + jnp.dot(
            jnp.concatenate(sides, axis=1), jnp.concatenate(weights, axis=0), preferred_element_type=F32
        )
        acc[at, :] = value
        return value

    first = 0
    while first < chunks - 1:
        group = list(range(first, min(first + 2, chunks - 1)))
        for chunk in group:
            drain(recv2.at[chunk], r2_sem.at[chunk])

        @pl.loop(0, tiles)
        def _(m):
            add_epipolar(group, m)

        first += len(group)

    def partial(i, carry):
        return carry + fold_rows(acc[pl.ds(pl.multiple_of(i * 64, 64), 64), :])

    summed = lax.fori_loop(0, rows // 64, partial, zeros)
    stats[0:1, :] = group_mean(jnp.sum(summed, axis=0, keepdims=True), collect, spread, members)

    drain(recv2.at[chunks - 1], r2_sem.at[chunks - 1])

    width = 256
    spans = channels // width
    lasts = [left(recv2, [chunks - 1], side, m) for m in range(tiles) for side in range(halves)]
    first = (chunks - 1) * LANES
    sums = []
    for n in range(spans):
        columns = slice(n * width, (n + 1) * width)
        weights = [
            merge_w[channels + side * half + first : channels + side * half + first + LANES, columns]
            for side in range(halves)
        ]
        weights = jnp.concatenate(weights, axis=0)
        middle = stats[0:1, columns]
        summed = jnp.zeros((ROWS, width), F32)
        squares = jnp.zeros((ROWS, width), F32)
        for m in range(tiles):
            at = slice(m * tile, (m + 1) * tile)
            inputs = jnp.concatenate(lasts[halves * m : halves * (m + 1)], axis=1)
            difference = acc[at, columns] - middle + jnp.dot(inputs, weights, preferred_element_type=F32)
            acc[at, columns] = difference
            summed = summed + fold_rows(difference)
            squares = squares + fold_rows(difference * difference)
        sums.append((summed, squares))
    rows_of = [
        jnp.sum(jnp.concatenate([pair[i] for pair in sums], axis=1), axis=0, keepdims=True) for i in range(2)
    ]
    moved, square = [total / members for total in exact_rows(rows_of, collect)]
    scale = lax.rsqrt(jnp.maximum(square - moved * moved, 0.0) + 1e-05)
    moved, scale = exact_rows([moved, scale], spread)
    stats[0:1, :] = moved
    stats[1:2, :] = scale

    def activate(m, n):
        at, columns = slice(m * tile, (m + 1) * tile), slice(n * width, (n + 1) * width)
        value = silu((acc[at, columns] - stats[0:1, columns]) * stats[1:2, columns])
        act[at, columns] = value.astype(BF16)

    for n in range(spans):
        activate(0, n)
    for m in range(tiles):
        at = slice(m * tile, (m + 1) * tile)
        for n in range(spans):
            columns = slice(n * width, (n + 1) * width)
            projected = jnp.dot(act[at, :], out_w[:, columns], preferred_element_type=F32)
            if m + 1 < tiles:
                activate(m + 1, n)
            for pair in range(tile_strips // 2):
                top = 2 * pair * slice_rows
                for block in range(blocks):
                    upper = projected[top + block * ROWS : top + (block + 1) * ROWS]
                    lower = projected[top + slice_rows + block * ROWS : top + slice_rows + (block + 1) * ROWS]
                    start = block * BLOCK + m * (tile_strips * ROWS) + pair * 2 * ROWS
                    to = slice(start, start + 2 * ROWS)
                    value = x[to, columns].astype(F32) + jnp.concatenate([upper, lower], axis=0)
                    out_ref[to, columns] = value.astype(BF16)

    for chunk in range(chunks):
        drain(send1.at[chunk, pl.ds(0, shards - 1)], s1_sem.at[chunk])
        drain(send2.at[chunk, pl.ds(0, shards - 1)], s2_sem.at[chunk])
    drain(full.at[pl.ds(0, zs - 1), 0], ws_sem.at[0])
    drain(full.at[pl.ds(0, (ys - 1) * zs), 0], ws_sem.at[1])
    drain(full.at[pl.ds(0, (xs - 1) * shards // pieces)], ws_sem.at[2])
    drain(full.at[pl.ds(0, xs * shards // pieces)], ws_sem.at[3])


def solution(mesh):
    sizes = (4, 8, 4, 2)

    def per_device(features, norm_gain, norm_shift, merge_weight, out_weight, corr_src, corr_count):
        rows, channels = features.shape
        shards = lax.axis_size("shard")
        groups = lax.axis_size("grp")
        slice_rows = rows // BLOCK * ROWS
        chunks = channels // (shards // (BLOCK // ROWS)) // LANES
        hbm = pl.BlockSpec(memory_space=pltpu.HBM)
        slices = pltpu.VMEM((chunks, shards, slice_rows, LANES), BF16)
        dma = pltpu.SemaphoreType.DMA
        return pl.pallas_call(
            functools.partial(kernel, sizes),
            out_shape=pltpu.VMEM(features.shape, features.dtype),
            in_specs=[hbm] * 7,
            out_specs=pl.BlockSpec(memory_space=pltpu.VMEM),
            scratch_shapes=[
                pltpu.VMEM((rows, channels), BF16),
                pltpu.VMEM((ROWS, channels), F32),
                pltpu.VMEM(merge_weight.shape, BF16),
                pltpu.VMEM(out_weight.shape, BF16),
                pltpu.SMEM(corr_src.shape[::-1], jnp.int32),
                pltpu.SMEM(corr_count.shape, jnp.int32),
                pltpu.VMEM((groups, PIECE, channels), BF16),
                slices, slices, slices, slices,
                pltpu.VMEM((corr_src.shape[0], ROWS, LANES), F32),
                pltpu.VMEM((shards, groups, PIECE, channels), BF16),
                pltpu.VMEM((2 * channels, channels), BF16),
                pltpu.VMEM((channels, channels), BF16),
                pltpu.VMEM((rows, channels), F32),
                pltpu.VMEM((rows, channels), BF16),
                pltpu.VMEM((channels, LANES), BF16),
                pltpu.VMEM((LANES, channels), BF16),
                pltpu.VMEM((ROWS, channels), F32),
                dma((7,)),
                dma((chunks,)), dma((chunks,)), dma((chunks,)), dma((chunks,)),
                dma((4,)), dma((4,)),
            ],
            compiler_params=pltpu.CompilerParams(
                collective_id=0, has_side_effects=True, vmem_limit_bytes=44 * 1024 * 1024
            ),
            name="merge_block",
        )(
            *(
                pltpu.with_memory_space_constraint(array, pltpu.HBM)
                for array in (
                    features, norm_gain, norm_shift, merge_weight, out_weight, corr_src.T, corr_count
                )
            )
        )

    placed = (
        P(("grp", "shard"), None),
        P(),
        P(),
        P("shard", None),
        P("shard", None),
        P("grp", None),
        P("grp"),
    )
    return jax.shard_map(
        per_device, mesh=mesh, in_specs=placed, out_specs=P(("grp", "shard"), None), check_vma=False
    )
```

```python
import functools

import jax
import jax.numpy as jnp
from jax import lax
from jax.experimental import pallas as pl
from jax.experimental.pallas import tpu as pltpu
from jax.sharding import PartitionSpec as P

GROUPS = 32
BLOCK = 128
LANES = 128
ROWS = 8
PIECE = 16
MESH = pl.DeviceIdType.MESH
F32 = jnp.float32
BF16 = jnp.bfloat16


def zigzag(center, place):
    odd = place % 2
    return center + (1 - odd) * (place // 2) - odd * ((place + 1) // 2)


def exact_rows(rows, matrix):
    parts = []
    for row in rows:
        high = row.astype(BF16).astype(F32)
        rest = row - high
        middle = rest.astype(BF16).astype(F32)
        parts += [high, middle, rest - middle]
    parts.append(jnp.zeros((PIECE - len(parts), rows[0].shape[1]), F32))
    stacked = jnp.concatenate(parts, axis=0).astype(BF16)
    product = jnp.dot(stacked, matrix[...], preferred_element_type=F32)
    return [product[i : i + 1] + product[i + 1 : i + 2] + product[i + 2 : i + 3] for i in range(0, 3 * len(rows), 3)]


def group_mean(row, collect, spread, members):
    (total,) = exact_rows([row], collect)
    return exact_rows([total / members], spread)[0]


def fold_rows(values):
    return jnp.sum(values.reshape(values.shape[0] // ROWS, ROWS, values.shape[1]), axis=0)


def silu(values):
    middle = 0.5 * values
    return middle + middle * jnp.tanh(middle)


def kernel(
    sizes,
    x_hbm, gain_hbm, shift_hbm, merge_hbm, outw_hbm, src_hbm, count_hbm,
    out_ref,
    x, params, merge_ref, outw_ref, src_ref, count_ref, stage, send1, recv1, send2, recv2, table, full, merge_w, out_w, acc, act, collect, spread, stats,
    load_sem, s1_sem, r1_sem, s2_sem, r2_sem, ws_sem, wr_sem,
):
    ys, zs, xs, cores = sizes
    shards = ys * zs
    rows, channels = x.shape
    blocks = rows // BLOCK
    strips = BLOCK // ROWS
    halves = shards // strips
    half = channels // halves
    chunks = half // LANES
    pieces = full.shape[1]
    merge_rows = merge_ref.shape[0]
    out_rows = outw_ref.shape[0]
    merge_pieces = merge_rows // PIECE
    group_width = channels // GROUPS
    members = float(rows * group_width)
    slice_rows = blocks * ROWS

    s = lax.axis_index("shard")
    g = lax.axis_index("grp")
    y, z = s // zs, s % zs
    xx, core = g // cores, g % cores

    load = pltpu.make_async_copy(x_hbm, x, load_sem.at[0])
    load.start()
    fetches = [
        pltpu.make_async_copy(source, target, load_sem.at[1 + i])
        for i, (source, target) in enumerate(
            (
                (merge_hbm, merge_ref), (outw_hbm, outw_ref), (gain_hbm, params.at[0]), (shift_hbm, params.at[1]),
                (src_hbm, src_ref), (count_hbm, count_ref),
            )
        )
    ]
    for fetch in fetches:
        fetch.start()

    def peer_of(step):
        dz = zigzag(zs // 2, step // ys)
        dy = zigzag(ys // 2, step % ys)
        return ((y + dy) % ys) * zs + (z + dz) % zs

    barrier = pltpu.get_barrier_semaphore()

    @pl.loop(0, shards - 1)
    def _(step):
        pl.semaphore_signal(barrier, inc=1, device_id=(g, peer_of(step)), device_id_type=MESH)

    for dx in range(1, xs):
        to = ((xx + dx) % xs) * cores + core
        pl.semaphore_signal(barrier, inc=1, device_id=(to, s), device_id_type=MESH)
    sibling = xx * cores + (core + 1) % cores
    pl.semaphore_signal(barrier, inc=1, device_id=(sibling, s), device_id_type=MESH)

    lane = lax.broadcasted_iota(jnp.int32, (channels, LANES), 1) * group_width
    row = lax.broadcasted_iota(jnp.int32, (channels, LANES), 0)
    collect[...] = jnp.where((row >= lane) & (row < lane + group_width), 1.0, 0.0).astype(BF16)
    lane = lax.broadcasted_iota(jnp.int32, (LANES, channels), 1)
    row = lax.broadcasted_iota(jnp.int32, (LANES, channels), 0) * group_width
    spread[...] = jnp.where((lane >= row) & (lane < row + group_width), 1.0, 0.0).astype(BF16)

    def weight_copy(source, target, stage_no, to):
        return pltpu.make_async_remote_copy(
            src_ref=source, dst_ref=target, send_sem=ws_sem.at[stage_no], recv_sem=wr_sem.at[stage_no],
            device_id=to, device_id_type=MESH,
        )

    def drain(ref, sem):
        pltpu.make_async_copy(ref, ref, sem).wait()

    load.wait()

    def total(i, carry):
        part = x[pl.ds(pl.multiple_of(i * 64, 64), 64), :].astype(F32)
        return carry + fold_rows(part)

    zeros = jnp.zeros((ROWS, channels), F32)
    summed = lax.fori_loop(0, rows // 64, total, zeros)
    average = group_mean(jnp.sum(summed, axis=0, keepdims=True), collect, spread, members)

    def total_square(i, carry):
        part = x[pl.ds(pl.multiple_of(i * 64, 64), 64), :].astype(F32) - average
        return carry + fold_rows(part * part)

    summed = lax.fori_loop(0, rows // 64, total_square, zeros)
    variance = group_mean(jnp.sum(summed, axis=0, keepdims=True), collect, spread, members)
    stats[0:1, :] = average
    fetches[2].wait()
    fetches[3].wait()
    stats[1:2, :] = lax.rsqrt(variance + 1e-05) * params[0:1, :]
    stats[2:3, :] = params[1:2, :]

    def own_slice(source, target, chunk, recv_sem):
        pltpu.make_async_copy(source.at[chunk, s], target.at[chunk, s], recv_sem.at[chunk]).start()

    def exchange(source, target, chunk, send_sem, recv_sem, start, stop):
        @pl.loop(start, stop)
        def _(step):
            to = peer_of(step)
            pltpu.make_async_remote_copy(
                src_ref=source.at[chunk, to], dst_ref=target.at[chunk, s],
                send_sem=send_sem.at[chunk], recv_sem=recv_sem.at[chunk],
                device_id=(g, to), device_id_type=MESH,
            ).start()

    def hide(chunk):
        @pl.loop(0, strips // 2)
        def _(pair):
            for side in range(halves):
                lanes = pl.ds(pl.multiple_of(side * half + chunk * LANES, LANES), LANES)
                average = stats[0:1, lanes]
                scale = stats[1:2, lanes]
                shift = stats[2:3, lanes]
                upper, lower = [], []
                for block in range(blocks):
                    at = pl.ds(pl.multiple_of(block * BLOCK + pair * 16, 16), 16)
                    value = silu((x[at, lanes].astype(F32) - average) * scale + shift)
                    upper.append(value[0:ROWS])
                    lower.append(value[ROWS : 2 * ROWS])
                send1[chunk, side * strips + 2 * pair] = jnp.concatenate(upper, axis=0).astype(BF16)
                send1[chunk, side * strips + 2 * pair + 1] = jnp.concatenate(lower, axis=0).astype(BF16)

    fetches[0].wait()
    fetches[1].wait()

    for piece in range(merge_pieces):
        stage[piece] = merge_ref[piece * PIECE : (piece + 1) * PIECE, :]
    whole = out_rows // PIECE
    for piece in range(whole):
        stage[merge_pieces + piece] = outw_ref[piece * PIECE : (piece + 1) * PIECE, :]
    rest = out_rows - whole * PIECE
    tail = outw_ref[whole * PIECE : out_rows, :].astype(F32)
    stage[merge_pieces + whole] = jnp.concatenate(
        [tail, jnp.zeros((PIECE - rest, channels), F32)], axis=0
    ).astype(BF16)

    hide(0)
    pl.semaphore_wait(barrier, shards - 1 + xs - 1 + 1)

    def beside(dz):
        return y * zs + (z + dz + zs) % zs

    pltpu.make_async_copy(stage.at[g], full.at[s, g], wr_sem.at[0]).start()
    for dz in (-2, 2, -1, 1):
        weight_copy(stage.at[g], full.at[s, g], 0, (g, beside(dz))).start()

    early = shards // 4
    own_slice(send1, recv1, 0, r1_sem)
    exchange(send1, recv1, 0, s1_sem, r1_sem, 0, early)

    drain(full.at[pl.ds(0, 5), 0], wr_sem.at[0])
    way = 1 - 2 * core
    onward = full.at[beside(-2 * way), g]
    weight_copy(onward, onward, 4, (g, beside(2 * way))).start()
    for dz in (-1, 1):
        onward = full.at[beside(-2 * dz), g]
        weight_copy(onward, onward, 4, (g, beside(dz))).start()

    exchange(send1, recv1, 0, s1_sem, r1_sem, early, shards - 1)

    @pl.loop(1, chunks)
    def _(chunk):
        hide(chunk)
        own_slice(send1, recv1, chunk, r1_sem)
        exchange(send1, recv1, chunk, s1_sem, r1_sem, 0, shards - 1)

    drain(full.at[pl.ds(0, 3), 0], wr_sem.at[4])
    mine = full.at[pl.ds(y * zs, zs), g]
    for step in range(ys - 1):
        dy = zigzag(ys // 2, step)
        weight_copy(mine, mine, 1, (g, ((y + dy) % ys) * zs + z)).start()

    def gather(chunk):
        drain(recv1.at[chunk], r1_sem.at[chunk])

        @pl.loop(0, shards)
        def _(view):
            table[pl.ds(view * blocks, blocks)] = recv1[chunk, view].astype(F32).reshape(blocks, ROWS, LANES)

        @pl.loop(0, shards)
        def _(view):
            parts = []
            for block in range(blocks):
                k = view * blocks + block
                count = count_ref[k]
                second = jnp.where(count > 1, 1.0, 0.0).astype(F32)
                third = jnp.where(count > 2, 1.0, 0.0).astype(F32)
                share = jnp.where(count > 2, 1.0 / 3.0, jnp.where(count > 1, 0.5, 1.0)).astype(F32)
                value = table[src_ref[0, k]] + table[src_ref[1, k]] * second + table[src_ref[2, k]] * third
                parts.append(value * share)
            send2[chunk, view] = jnp.concatenate(parts, axis=0).astype(BF16)

        own_slice(send2, recv2, chunk, r2_sem)
        exchange(send2, recv2, chunk, s2_sem, r2_sem, 0, shards - 1)

    fetches[4].wait()
    fetches[5].wait()
    gather(0)

    drain(full.at[pl.ds(0, (ys - 1) * zs), 0], wr_sem.at[1])
    mine = full.at[:, g]
    for step in range(xs - 1):
        dx = zigzag(xs // 2, step)
        weight_copy(mine, mine, 2, (((xx + dx) % xs) * cores + core, s)).start()
    weight_copy(mine, mine, 3, (sibling, s)).start()

    @pl.loop(1, chunks)
    def _(chunk):
        gather(chunk)

    drain(full.at[pl.ds(0, (xs - 1) * shards // pieces)], wr_sem.at[2])
    for dx in range(1, xs):
        theirs = full.at[:, ((xx + dx) % xs) * cores + core]
        weight_copy(theirs, theirs, 3, (sibling, s)).start()
    drain(full.at[pl.ds(0, xs * shards // pieces)], wr_sem.at[3])

    @pl.loop(0, shards)
    def _(shard):
        for piece in range(merge_pieces):
            at = pl.ds(pl.multiple_of(shard * merge_rows + piece * PIECE, PIECE), PIECE)
            merge_w[at, :] = full[shard, piece]

    @pl.loop(0, shards // 2)
    def _(pair):
        parts = []
        for member in range(2):
            for piece in range(whole + 1):
                part = full[2 * pair + member, merge_pieces + piece].astype(F32)
                parts.append(part if piece < whole else part[0:rest])
        at = pl.ds(pl.multiple_of(pair * 2 * out_rows, PIECE), 2 * out_rows)
        out_w[at, :] = jnp.concatenate(parts, axis=0).astype(BF16)

    tile = 256
    tile_strips = tile // slice_rows
    tiles = rows // tile

    def left(ref, chunk_list, side, m):
        at = pl.ds(side * strips + m * tile_strips, tile_strips)
        return jnp.concatenate([ref[chunk, at].reshape(tile, LANES) for chunk in chunk_list], axis=1)

    @pl.loop(0, tiles)
    def _(m):
        sides = [left(send1, range(chunks), side, m) for side in range(halves)]
        at = pl.ds(pl.multiple_of(m * tile, tile), tile)
        acc[at, :] = jnp.dot(
            jnp.concatenate(sides, axis=1), merge_w[0:channels, :], preferred_element_type=F32
        )

    def add_epipolar(chunk_list, m):
        depth = len(chunk_list) * LANES
        first = chunk_list[0] * LANES
        sides = [left(recv2, chunk_list, side, m) for side in range(halves)]
        weights = [
            merge_w[channels + side * half + first : channels + side * half + first + depth, :]
            for side in range(halves)
        ]
        at = pl.ds(pl.multiple_of(m * tile, tile), tile)
        value = acc[at, :] + jnp.dot(
            jnp.concatenate(sides, axis=1), jnp.concatenate(weights, axis=0), preferred_element_type=F32
        )
        acc[at, :] = value
        return value

    first = 0
    while first < chunks - 1:
        group = list(range(first, min(first + 2, chunks - 1)))
        for chunk in group:
            drain(recv2.at[chunk], r2_sem.at[chunk])

        @pl.loop(0, tiles)
        def _(m):
            add_epipolar(group, m)

        first += len(group)

    def partial(i, carry):
        return carry + fold_rows(acc[pl.ds(pl.multiple_of(i * 64, 64), 64), :])

    summed = lax.fori_loop(0, rows // 64, partial, zeros)
    stats[0:1, :] = group_mean(jnp.sum(summed, axis=0, keepdims=True), collect, spread, members)

    drain(recv2.at[chunks - 1], r2_sem.at[chunks - 1])

    width = 256
    spans = channels // width
    lasts = [left(recv2, [chunks - 1], side, m) for m in range(tiles) for side in range(halves)]
    first = (chunks - 1) * LANES
    sums = []
    for n in range(spans):
        columns = slice(n * width, (n + 1) * width)
        weights = [
            merge_w[channels + side * half + first : channels + side * half + first + LANES, columns]
            for side in range(halves)
        ]
        weights = jnp.concatenate(weights, axis=0)
        middle = stats[0:1, columns]
        summed = jnp.zeros((ROWS, width), F32)
        squares = jnp.zeros((ROWS, width), F32)
        for m in range(tiles):
            at = slice(m * tile, (m + 1) * tile)
            inputs = jnp.concatenate(lasts[halves * m : halves * (m + 1)], axis=1)
            difference = acc[at, columns] - middle + jnp.dot(inputs, weights, preferred_element_type=F32)
            acc[at, columns] = difference
            summed = summed + fold_rows(difference)
            squares = squares + fold_rows(difference * difference)
        sums.append((summed, squares))
    rows_of = [
        jnp.sum(jnp.concatenate([pair[i] for pair in sums], axis=1), axis=0, keepdims=True) for i in range(2)
    ]
    moved, square = [total / members for total in exact_rows(rows_of, collect)]
    scale = lax.rsqrt(jnp.maximum(square - moved * moved, 0.0) + 1e-05)
    moved, scale = exact_rows([moved, scale], spread)
    stats[0:1, :] = moved
    stats[1:2, :] = scale

    def activate(m, n):
        at, columns = slice(m * tile, (m + 1) * tile), slice(n * width, (n + 1) * width)
        value = silu((acc[at, columns] - stats[0:1, columns]) * stats[1:2, columns])
        act[at, columns] = value.astype(BF16)

    for n in range(spans):
        activate(0, n)
    for m in range(tiles):
        at = slice(m * tile, (m + 1) * tile)
        for n in range(spans):
            columns = slice(n * width, (n + 1) * width)
            projected = jnp.dot(act[at, :], out_w[:, columns], preferred_element_type=F32)
            if m + 1 < tiles:
                activate(m + 1, n)
            for pair in range(tile_strips // 2):
                top = 2 * pair * slice_rows
                for block in range(blocks):
                    upper = projected[top + block * ROWS : top + (block + 1) * ROWS]
                    lower = projected[top + slice_rows + block * ROWS : top + slice_rows + (block + 1) * ROWS]
                    start = block * BLOCK + m * (tile_strips * ROWS) + pair * 2 * ROWS
                    to = slice(start, start + 2 * ROWS)
                    value = x[to, columns].astype(F32) + jnp.concatenate([upper, lower], axis=0)
                    out_ref[to, columns] = value.astype(BF16)

    for chunk in range(chunks):
        drain(send1.at[chunk, pl.ds(0, shards - 1)], s1_sem.at[chunk])
        drain(send2.at[chunk, pl.ds(0, shards - 1)], s2_sem.at[chunk])
    drain(full.at[pl.ds(0, 4), 0], ws_sem.at[0])
    drain(full.at[pl.ds(0, 3), 0], ws_sem.at[4])
    drain(full.at[pl.ds(0, (ys - 1) * zs), 0], ws_sem.at[1])
    drain(full.at[pl.ds(0, (xs - 1) * shards // pieces)], ws_sem.at[2])
    drain(full.at[pl.ds(0, xs * shards // pieces)], ws_sem.at[3])


def solution(mesh):
    sizes = (4, 8, 4, 2)

    def per_device(features, norm_gain, norm_shift, merge_weight, out_weight, corr_src, corr_count):
        rows, channels = features.shape
        shards = lax.axis_size("shard")
        groups = lax.axis_size("grp")
        slice_rows = rows // BLOCK * ROWS
        chunks = channels // (shards // (BLOCK // ROWS)) // LANES
        hbm = pl.BlockSpec(memory_space=pltpu.HBM)
        slices = pltpu.VMEM((chunks, shards, slice_rows, LANES), BF16)
        dma = pltpu.SemaphoreType.DMA
        return pl.pallas_call(
            functools.partial(kernel, sizes),
            out_shape=pltpu.VMEM(features.shape, features.dtype),
            in_specs=[hbm] * 7,
            out_specs=pl.BlockSpec(memory_space=pltpu.VMEM),
            scratch_shapes=[
                pltpu.VMEM((rows, channels), BF16),
                pltpu.VMEM((ROWS, channels), F32),
                pltpu.VMEM(merge_weight.shape, BF16),
                pltpu.VMEM(out_weight.shape, BF16),
                pltpu.SMEM(corr_src.shape[::-1], jnp.int32),
                pltpu.SMEM(corr_count.shape, jnp.int32),
                pltpu.VMEM((groups, PIECE, channels), BF16),
                slices, slices, slices, slices,
                pltpu.VMEM((corr_src.shape[0], ROWS, LANES), F32),
                pltpu.VMEM((shards, groups, PIECE, channels), BF16),
                pltpu.VMEM((2 * channels, channels), BF16),
                pltpu.VMEM((channels, channels), BF16),
                pltpu.VMEM((rows, channels), F32),
                pltpu.VMEM((rows, channels), BF16),
                pltpu.VMEM((channels, LANES), BF16),
                pltpu.VMEM((LANES, channels), BF16),
                pltpu.VMEM((ROWS, channels), F32),
                dma((7,)),
                dma((chunks,)), dma((chunks,)), dma((chunks,)), dma((chunks,)),
                dma((5,)), dma((5,)),
            ],
            compiler_params=pltpu.CompilerParams(
                collective_id=0, has_side_effects=True, vmem_limit_bytes=44 * 1024 * 1024
            ),
            name="merge_block",
        )(
            *(
                pltpu.with_memory_space_constraint(array, pltpu.HBM)
                for array in (
                    features, norm_gain, norm_shift, merge_weight, out_weight, corr_src.T, corr_count
                )
            )
        )

    placed = (
        P(("grp", "shard"), None),
        P(),
        P(),
        P("shard", None),
        P("shard", None),
        P("grp", None),
        P("grp"),
    )
    return jax.shard_map(
        per_device, mesh=mesh, in_specs=placed, out_specs=P(("grp", "shard"), None), check_vma=False
    )
```

```python
import functools

import jax
import jax.numpy as jnp
from jax import lax
from jax.experimental import pallas as pl
from jax.experimental.pallas import tpu as pltpu
from jax.sharding import PartitionSpec as P

GROUPS = 32
BLOCK = 128
LANES = 128
ROWS = 8
PIECE = 16
MESH = pl.DeviceIdType.MESH
F32 = jnp.float32
BF16 = jnp.bfloat16


def zigzag(center, place):
    odd = place % 2
    return center + (1 - odd) * (place // 2) - odd * ((place + 1) // 2)


def exact_rows(rows, matrix):
    parts = []
    for row in rows:
        high = row.astype(BF16).astype(F32)
        rest = row - high
        middle = rest.astype(BF16).astype(F32)
        parts += [high, middle, rest - middle]
    parts.append(jnp.zeros((PIECE - len(parts), rows[0].shape[1]), F32))
    stacked = jnp.concatenate(parts, axis=0).astype(BF16)
    product = jnp.dot(stacked, matrix[...], preferred_element_type=F32)
    return [product[i : i + 1] + product[i + 1 : i + 2] + product[i + 2 : i + 3] for i in range(0, 3 * len(rows), 3)]


def group_mean(row, collect, spread, members):
    (total,) = exact_rows([row], collect)
    return exact_rows([total / members], spread)[0]


def fold_rows(values):
    return jnp.sum(values.reshape(values.shape[0] // ROWS, ROWS, values.shape[1]), axis=0)


def silu(values):
    middle = 0.5 * values
    return middle + middle * jnp.tanh(middle)


def kernel(
    sizes,
    x_hbm, gain_hbm, shift_hbm, merge_hbm, outw_hbm, src_hbm, count_hbm,
    out_ref,
    x, params, merge_ref, outw_ref, src_ref, count_ref, stage, send1, recv1, send2, recv2, table, full, merge_w, out_w, acc, act, collect, spread, stats,
    load_sem, s1_sem, r1_sem, s2_sem, r2_sem, ws_sem, wr_sem,
):
    ys, zs, xs, cores = sizes
    shards = ys * zs
    rows, channels = x.shape
    blocks = rows // BLOCK
    strips = BLOCK // ROWS
    halves = shards // strips
    half = channels // halves
    chunks = half // LANES
    pieces = full.shape[1]
    merge_rows = merge_ref.shape[0]
    out_rows = outw_ref.shape[0]
    merge_pieces = merge_rows // PIECE
    group_width = channels // GROUPS
    members = float(rows * group_width)
    slice_rows = blocks * ROWS

    s = lax.axis_index("shard")
    g = lax.axis_index("grp")
    y, z = s // zs, s % zs
    xx, core = g // cores, g % cores

    load = pltpu.make_async_copy(x_hbm, x, load_sem.at[0])
    load.start()
    fetches = [
        pltpu.make_async_copy(source, target, load_sem.at[1 + i])
        for i, (source, target) in enumerate(
            (
                (merge_hbm, merge_ref), (outw_hbm, outw_ref), (gain_hbm, params.at[0]), (shift_hbm, params.at[1]),
                (src_hbm, src_ref), (count_hbm, count_ref),
            )
        )
    ]
    for fetch in fetches:
        fetch.start()

    def peer_of(step):
        dz = zigzag(zs // 2, step // ys)
        dy = zigzag(ys // 2, step % ys)
        return ((y + dy) % ys) * zs + (z + dz) % zs

    barrier = pltpu.get_barrier_semaphore()

    @pl.loop(0, shards - 1)
    def _(step):
        pl.semaphore_signal(barrier, inc=1, device_id=(g, peer_of(step)), device_id_type=MESH)

    for dx in range(1, xs):
        to = ((xx + dx) % xs) * cores + core
        pl.semaphore_signal(barrier, inc=1, device_id=(to, s), device_id_type=MESH)
    sibling = xx * cores + (core + 1) % cores
    pl.semaphore_signal(barrier, inc=1, device_id=(sibling, s), device_id_type=MESH)

    lane = lax.broadcasted_iota(jnp.int32, (channels, LANES), 1) * group_width
    row = lax.broadcasted_iota(jnp.int32, (channels, LANES), 0)
    collect[...] = jnp.where((row >= lane) & (row < lane + group_width), 1.0, 0.0).astype(BF16)
    lane = lax.broadcasted_iota(jnp.int32, (LANES, channels), 1)
    row = lax.broadcasted_iota(jnp.int32, (LANES, channels), 0) * group_width
    spread[...] = jnp.where((lane >= row) & (lane < row + group_width), 1.0, 0.0).astype(BF16)

    def weight_copy(source, target, stage_no, to):
        return pltpu.make_async_remote_copy(
            src_ref=source, dst_ref=target, send_sem=ws_sem.at[stage_no], recv_sem=wr_sem.at[stage_no],
            device_id=to, device_id_type=MESH,
        )

    def drain(ref, sem):
        pltpu.make_async_copy(ref, ref, sem).wait()

    fetches[0].wait()
    fetches[1].wait()

    for piece in range(merge_pieces):
        stage[piece] = merge_ref[piece * PIECE : (piece + 1) * PIECE, :]
    whole = out_rows // PIECE
    for piece in range(whole):
        stage[merge_pieces + piece] = outw_ref[piece * PIECE : (piece + 1) * PIECE, :]
    rest = out_rows - whole * PIECE
    tail = outw_ref[whole * PIECE : out_rows, :].astype(F32)
    stage[merge_pieces + whole] = jnp.concatenate(
        [tail, jnp.zeros((PIECE - rest, channels), F32)], axis=0
    ).astype(BF16)

    pl.semaphore_wait(barrier, shards - 1 + xs - 1 + 1)

    def beside(dz):
        return y * zs + (z + dz + zs) % zs

    pltpu.make_async_copy(stage.at[g], full.at[s, g], wr_sem.at[0]).start()
    for dz in (-2, 2, -1, 1):
        weight_copy(stage.at[g], full.at[s, g], 0, (g, beside(dz))).start()

    load.wait()

    def total(i, carry):
        part = x[pl.ds(pl.multiple_of(i * 64, 64), 64), :].astype(F32)
        return carry + fold_rows(part)

    zeros = jnp.zeros((ROWS, channels), F32)
    summed = lax.fori_loop(0, rows // 64, total, zeros)
    average = group_mean(jnp.sum(summed, axis=0, keepdims=True), collect, spread, members)

    def total_square(i, carry):
        part = x[pl.ds(pl.multiple_of(i * 64, 64), 64), :].astype(F32) - average
        return carry + fold_rows(part * part)

    summed = lax.fori_loop(0, rows // 64, total_square, zeros)
    variance = group_mean(jnp.sum(summed, axis=0, keepdims=True), collect, spread, members)
    stats[0:1, :] = average
    fetches[2].wait()
    fetches[3].wait()
    stats[1:2, :] = lax.rsqrt(variance + 1e-05) * params[0:1, :]
    stats[2:3, :] = params[1:2, :]

    def own_slice(source, target, chunk, recv_sem):
        pltpu.make_async_copy(source.at[chunk, s], target.at[chunk, s], recv_sem.at[chunk]).start()

    def exchange(source, target, chunk, send_sem, recv_sem, start, stop):
        @pl.loop(start, stop)
        def _(step):
            to = peer_of(step)
            pltpu.make_async_remote_copy(
                src_ref=source.at[chunk, to], dst_ref=target.at[chunk, s],
                send_sem=send_sem.at[chunk], recv_sem=recv_sem.at[chunk],
                device_id=(g, to), device_id_type=MESH,
            ).start()

    def hide(chunk):
        @pl.loop(0, strips // 2)
        def _(pair):
            for side in range(halves):
                lanes = pl.ds(pl.multiple_of(side * half + chunk * LANES, LANES), LANES)
                average = stats[0:1, lanes]
                scale = stats[1:2, lanes]
                shift = stats[2:3, lanes]
                upper, lower = [], []
                for block in range(blocks):
                    at = pl.ds(pl.multiple_of(block * BLOCK + pair * 16, 16), 16)
                    value = silu((x[at, lanes].astype(F32) - average) * scale + shift)
                    upper.append(value[0:ROWS])
                    lower.append(value[ROWS : 2 * ROWS])
                send1[chunk, side * strips + 2 * pair] = jnp.concatenate(upper, axis=0).astype(BF16)
                send1[chunk, side * strips + 2 * pair + 1] = jnp.concatenate(lower, axis=0).astype(BF16)

    hide(0)
    early = shards // 4
    own_slice(send1, recv1, 0, r1_sem)
    exchange(send1, recv1, 0, s1_sem, r1_sem, 0, early)

    drain(full.at[pl.ds(0, 5), 0], wr_sem.at[0])
    way = 1 - 2 * core
    onward = full.at[beside(-2 * way), g]
    weight_copy(onward, onward, 4, (g, beside(2 * way))).start()
    for dz in (-1, 1):
        onward = full.at[beside(-2 * dz), g]
        weight_copy(onward, onward, 4, (g, beside(dz))).start()

    exchange(send1, recv1, 0, s1_sem, r1_sem, early, shards - 1)

    @pl.loop(1, chunks)
    def _(chunk):
        hide(chunk)
        own_slice(send1, recv1, chunk, r1_sem)
        exchange(send1, recv1, chunk, s1_sem, r1_sem, 0, shards - 1)

    drain(full.at[pl.ds(0, 3), 0], wr_sem.at[4])
    mine = full.at[pl.ds(y * zs, zs), g]
    for step in range(ys - 1):
        dy = zigzag(ys // 2, step)
        weight_copy(mine, mine, 1, (g, ((y + dy) % ys) * zs + z)).start()

    def gather(chunk):
        drain(recv1.at[chunk], r1_sem.at[chunk])

        @pl.loop(0, shards)
        def _(view):
            table[pl.ds(view * blocks, blocks)] = recv1[chunk, view].astype(F32).reshape(blocks, ROWS, LANES)

        @pl.loop(0, shards)
        def _(view):
            parts = []
            for block in range(blocks):
                k = view * blocks + block
                count = count_ref[k]
                second = jnp.where(count > 1, 1.0, 0.0).astype(F32)
                third = jnp.where(count > 2, 1.0, 0.0).astype(F32)
                share = jnp.where(count > 2, 1.0 / 3.0, jnp.where(count > 1, 0.5, 1.0)).astype(F32)
                value = table[src_ref[0, k]] + table[src_ref[1, k]] * second + table[src_ref[2, k]] * third
                parts.append(value * share)
            send2[chunk, view] = jnp.concatenate(parts, axis=0).astype(BF16)

        own_slice(send2, recv2, chunk, r2_sem)
        exchange(send2, recv2, chunk, s2_sem, r2_sem, 0, shards - 1)

    fetches[4].wait()
    fetches[5].wait()
    gather(0)

    drain(full.at[pl.ds(0, (ys - 1) * zs), 0], wr_sem.at[1])
    mine = full.at[:, g]
    for step in range(xs - 1):
        dx = zigzag(xs // 2, step)
        weight_copy(mine, mine, 2, (((xx + dx) % xs) * cores + core, s)).start()
    weight_copy(mine, mine, 3, (sibling, s)).start()

    @pl.loop(1, chunks)
    def _(chunk):
        gather(chunk)

    drain(full.at[pl.ds(0, (xs - 1) * shards // pieces)], wr_sem.at[2])
    for dx in range(1, xs):
        theirs = full.at[:, ((xx + dx) % xs) * cores + core]
        weight_copy(theirs, theirs, 3, (sibling, s)).start()
    drain(full.at[pl.ds(0, xs * shards // pieces)], wr_sem.at[3])

    @pl.loop(0, shards)
    def _(shard):
        for piece in range(merge_pieces):
            at = pl.ds(pl.multiple_of(shard * merge_rows + piece * PIECE, PIECE), PIECE)
            merge_w[at, :] = full[shard, piece]

    @pl.loop(0, shards // 2)
    def _(pair):
        parts = []
        for member in range(2):
            for piece in range(whole + 1):
                part = full[2 * pair + member, merge_pieces + piece].astype(F32)
                parts.append(part if piece < whole else part[0:rest])
        at = pl.ds(pl.multiple_of(pair * 2 * out_rows, PIECE), 2 * out_rows)
        out_w[at, :] = jnp.concatenate(parts, axis=0).astype(BF16)

    tile = 256
    tile_strips = tile // slice_rows
    tiles = rows // tile

    def left(ref, chunk_list, side, m):
        at = pl.ds(side * strips + m * tile_strips, tile_strips)
        return jnp.concatenate([ref[chunk, at].reshape(tile, LANES) for chunk in chunk_list], axis=1)

    @pl.loop(0, tiles)
    def _(m):
        sides = [left(send1, range(chunks), side, m) for side in range(halves)]
        at = pl.ds(pl.multiple_of(m * tile, tile), tile)
        acc[at, :] = jnp.dot(
            jnp.concatenate(sides, axis=1), merge_w[0:channels, :], preferred_element_type=F32
        )

    def add_epipolar(chunk_list, m):
        depth = len(chunk_list) * LANES
        first = chunk_list[0] * LANES
        sides = [left(recv2, chunk_list, side, m) for side in range(halves)]
        weights = [
            merge_w[channels + side * half + first : channels + side * half + first + depth, :]
            for side in range(halves)
        ]
        at = pl.ds(pl.multiple_of(m * tile, tile), tile)
        value = acc[at, :] + jnp.dot(
            jnp.concatenate(sides, axis=1), jnp.concatenate(weights, axis=0), preferred_element_type=F32
        )
        acc[at, :] = value
        return value

    first = 0
    while first < chunks - 1:
        group = list(range(first, min(first + 2, chunks - 1)))
        for chunk in group:
            drain(recv2.at[chunk], r2_sem.at[chunk])

        @pl.loop(0, tiles)
        def _(m):
            add_epipolar(group, m)

        first += len(group)

    def partial(i, carry):
        return carry + fold_rows(acc[pl.ds(pl.multiple_of(i * 64, 64), 64), :])

    summed = lax.fori_loop(0, rows // 64, partial, zeros)
    stats[0:1, :] = group_mean(jnp.sum(summed, axis=0, keepdims=True), collect, spread, members)

    drain(recv2.at[chunks - 1], r2_sem.at[chunks - 1])

    width = 256
    spans = channels // width
    lasts = [left(recv2, [chunks - 1], side, m) for m in range(tiles) for side in range(halves)]
    first = (chunks - 1) * LANES
    sums = []
    for n in range(spans):
        columns = slice(n * width, (n + 1) * width)
        weights = [
            merge_w[channels + side * half + first : channels + side * half + first + LANES, columns]
            for side in range(halves)
        ]
        weights = jnp.concatenate(weights, axis=0)
        middle = stats[0:1, columns]
        summed = jnp.zeros((ROWS, width), F32)
        squares = jnp.zeros((ROWS, width), F32)
        for m in range(tiles):
            at = slice(m * tile, (m + 1) * tile)
            inputs = jnp.concatenate(lasts[halves * m : halves * (m + 1)], axis=1)
            difference = acc[at, columns] - middle + jnp.dot(inputs, weights, preferred_element_type=F32)
            acc[at, columns] = difference
            summed = summed + fold_rows(difference)
            squares = squares + fold_rows(difference * difference)
        sums.append((summed, squares))
    rows_of = [
        jnp.sum(jnp.concatenate([pair[i] for pair in sums], axis=1), axis=0, keepdims=True) for i in range(2)
    ]
    moved, square = [total / members for total in exact_rows(rows_of, collect)]
    scale = lax.rsqrt(jnp.maximum(square - moved * moved, 0.0) + 1e-05)
    moved, scale = exact_rows([moved, scale], spread)
    stats[0:1, :] = moved
    stats[1:2, :] = scale

    def activate(m, n):
        at, columns = slice(m * tile, (m + 1) * tile), slice(n * width, (n + 1) * width)
        value = silu((acc[at, columns] - stats[0:1, columns]) * stats[1:2, columns])
        act[at, columns] = value.astype(BF16)

    for n in range(spans):
        activate(0, n)
    for m in range(tiles):
        at = slice(m * tile, (m + 1) * tile)
        for n in range(spans):
            columns = slice(n * width, (n + 1) * width)
            projected = jnp.dot(act[at, :], out_w[:, columns], preferred_element_type=F32)
            if m + 1 < tiles:
                activate(m + 1, n)
            for pair in range(tile_strips // 2):
                top = 2 * pair * slice_rows
                for block in range(blocks):
                    upper = projected[top + block * ROWS : top + (block + 1) * ROWS]
                    lower = projected[top + slice_rows + block * ROWS : top + slice_rows + (block + 1) * ROWS]
                    start = block * BLOCK + m * (tile_strips * ROWS) + pair * 2 * ROWS
                    to = slice(start, start + 2 * ROWS)
                    value = x[to, columns].astype(F32) + jnp.concatenate([upper, lower], axis=0)
                    out_ref[to, columns] = value.astype(BF16)

    for chunk in range(chunks):
        drain(send1.at[chunk, pl.ds(0, shards - 1)], s1_sem.at[chunk])
        drain(send2.at[chunk, pl.ds(0, shards - 1)], s2_sem.at[chunk])
    drain(full.at[pl.ds(0, 4), 0], ws_sem.at[0])
    drain(full.at[pl.ds(0, 3), 0], ws_sem.at[4])
    drain(full.at[pl.ds(0, (ys - 1) * zs), 0], ws_sem.at[1])
    drain(full.at[pl.ds(0, (xs - 1) * shards // pieces)], ws_sem.at[2])
    drain(full.at[pl.ds(0, xs * shards // pieces)], ws_sem.at[3])


def solution(mesh):
    sizes = (4, 8, 4, 2)

    def per_device(features, norm_gain, norm_shift, merge_weight, out_weight, corr_src, corr_count):
        rows, channels = features.shape
        shards = lax.axis_size("shard")
        groups = lax.axis_size("grp")
        slice_rows = rows // BLOCK * ROWS
        chunks = channels // (shards // (BLOCK // ROWS)) // LANES
        hbm = pl.BlockSpec(memory_space=pltpu.HBM)
        slices = pltpu.VMEM((chunks, shards, slice_rows, LANES), BF16)
        dma = pltpu.SemaphoreType.DMA
        return pl.pallas_call(
            functools.partial(kernel, sizes),
            out_shape=pltpu.VMEM(features.shape, features.dtype),
            in_specs=[hbm] * 7,
            out_specs=pl.BlockSpec(memory_space=pltpu.VMEM),
            scratch_shapes=[
                pltpu.VMEM((rows, channels), BF16),
                pltpu.VMEM((ROWS, channels), F32),
                pltpu.VMEM(merge_weight.shape, BF16),
                pltpu.VMEM(out_weight.shape, BF16),
                pltpu.SMEM(corr_src.shape[::-1], jnp.int32),
                pltpu.SMEM(corr_count.shape, jnp.int32),
                pltpu.VMEM((groups, PIECE, channels), BF16),
                slices, slices, slices, slices,
                pltpu.VMEM((corr_src.shape[0], ROWS, LANES), F32),
                pltpu.VMEM((shards, groups, PIECE, channels), BF16),
                pltpu.VMEM((2 * channels, channels), BF16),
                pltpu.VMEM((channels, channels), BF16),
                pltpu.VMEM((rows, channels), F32),
                pltpu.VMEM((rows, channels), BF16),
                pltpu.VMEM((channels, LANES), BF16),
                pltpu.VMEM((LANES, channels), BF16),
                pltpu.VMEM((ROWS, channels), F32),
                dma((7,)),
                dma((chunks,)), dma((chunks,)), dma((chunks,)), dma((chunks,)),
                dma((5,)), dma((5,)),
            ],
            compiler_params=pltpu.CompilerParams(
                collective_id=0, has_side_effects=True, vmem_limit_bytes=44 * 1024 * 1024
            ),
            name="merge_block",
        )(
            *(
                pltpu.with_memory_space_constraint(array, pltpu.HBM)
                for array in (
                    features, norm_gain, norm_shift, merge_weight, out_weight, corr_src.T, corr_count
                )
            )
        )

    placed = (
        P(("grp", "shard"), None),
        P(),
        P(),
        P("shard", None),
        P("shard", None),
        P("grp", None),
        P("grp"),
    )
    return jax.shard_map(
        per_device, mesh=mesh, in_specs=placed, out_specs=P(("grp", "shard"), None), check_vma=False
    )
```

```python
import functools

import jax
import jax.numpy as jnp
from jax import lax
from jax.experimental import pallas as pl
from jax.experimental.pallas import tpu as pltpu
from jax.sharding import PartitionSpec as P

GROUPS = 32
BLOCK = 128
LANES = 128
ROWS = 8
PIECE = 16
MESH = pl.DeviceIdType.MESH
F32 = jnp.float32
BF16 = jnp.bfloat16


def zigzag(center, place):
    odd = place % 2
    return center + (1 - odd) * (place // 2) - odd * ((place + 1) // 2)


def exact_rows(rows, matrix):
    parts = []
    for row in rows:
        high = row.astype(BF16).astype(F32)
        rest = row - high
        middle = rest.astype(BF16).astype(F32)
        parts += [high, middle, rest - middle]
    parts.append(jnp.zeros((PIECE - len(parts), rows[0].shape[1]), F32))
    stacked = jnp.concatenate(parts, axis=0).astype(BF16)
    product = jnp.dot(stacked, matrix[...], preferred_element_type=F32)
    return [product[i : i + 1] + product[i + 1 : i + 2] + product[i + 2 : i + 3] for i in range(0, 3 * len(rows), 3)]


def group_mean(row, collect, spread, members):
    (total,) = exact_rows([row], collect)
    return exact_rows([total / members], spread)[0]


def fold_rows(values):
    return jnp.sum(values.reshape(values.shape[0] // ROWS, ROWS, values.shape[1]), axis=0)


def silu(values):
    middle = 0.5 * values
    return middle + middle * jnp.tanh(middle)


def kernel(
    sizes,
    x_hbm, gain_hbm, shift_hbm, merge_hbm, outw_hbm, src_hbm, count_hbm,
    x, out_w, acc, stats,
    params, merge_ref, outw_ref, src_ref, count_ref, stage, send1, recv1, send2, recv2, table, full, merge_w, collect, spread,
    load_sem, s1_sem, r1_sem, s2_sem, r2_sem, ws_sem, wr_sem,
):
    ys, zs, xs, cores = sizes
    shards = ys * zs
    rows, channels = x.shape
    blocks = rows // BLOCK
    strips = BLOCK // ROWS
    halves = shards // strips
    half = channels // halves
    chunks = half // LANES
    pieces = full.shape[1]
    merge_rows = merge_ref.shape[0]
    out_rows = outw_ref.shape[0]
    merge_pieces = merge_rows // PIECE
    group_width = channels // GROUPS
    members = float(rows * group_width)
    slice_rows = blocks * ROWS

    s = lax.axis_index("shard")
    g = lax.axis_index("grp")
    y, z = s // zs, s % zs
    xx, core = g // cores, g % cores

    load = pltpu.make_async_copy(x_hbm, x, load_sem.at[0])
    load.start()
    fetches = [
        pltpu.make_async_copy(source, target, load_sem.at[1 + i])
        for i, (source, target) in enumerate(
            (
                (merge_hbm, merge_ref), (outw_hbm, outw_ref), (gain_hbm, params.at[0]), (shift_hbm, params.at[1]),
                (src_hbm, src_ref), (count_hbm, count_ref),
            )
        )
    ]
    for fetch in fetches:
        fetch.start()

    def peer_of(step):
        dz = zigzag(zs // 2, step // ys)
        dy = zigzag(ys // 2, step % ys)
        return ((y + dy) % ys) * zs + (z + dz) % zs

    barrier = pltpu.get_barrier_semaphore()

    @pl.loop(0, shards - 1)
    def _(step):
        pl.semaphore_signal(barrier, inc=1, device_id=(g, peer_of(step)), device_id_type=MESH)

    for dx in range(1, xs):
        to = ((xx + dx) % xs) * cores + core
        pl.semaphore_signal(barrier, inc=1, device_id=(to, s), device_id_type=MESH)
    sibling = xx * cores + (core + 1) % cores
    pl.semaphore_signal(barrier, inc=1, device_id=(sibling, s), device_id_type=MESH)

    lane = lax.broadcasted_iota(jnp.int32, (channels, LANES), 1) * group_width
    row = lax.broadcasted_iota(jnp.int32, (channels, LANES), 0)
    collect[...] = jnp.where((row >= lane) & (row < lane + group_width), 1.0, 0.0).astype(BF16)
    lane = lax.broadcasted_iota(jnp.int32, (LANES, channels), 1)
    row = lax.broadcasted_iota(jnp.int32, (LANES, channels), 0) * group_width
    spread[...] = jnp.where((lane >= row) & (lane < row + group_width), 1.0, 0.0).astype(BF16)

    def weight_copy(source, target, stage_no, to):
        return pltpu.make_async_remote_copy(
            src_ref=source, dst_ref=target, send_sem=ws_sem.at[stage_no], recv_sem=wr_sem.at[stage_no],
            device_id=to, device_id_type=MESH,
        )

    def drain(ref, sem):
        pltpu.make_async_copy(ref, ref, sem).wait()

    fetches[0].wait()
    fetches[1].wait()

    for piece in range(merge_pieces):
        stage[piece] = merge_ref[piece * PIECE : (piece + 1) * PIECE, :]
    whole = out_rows // PIECE
    for piece in range(whole):
        stage[merge_pieces + piece] = outw_ref[piece * PIECE : (piece + 1) * PIECE, :]
    rest = out_rows - whole * PIECE
    tail = outw_ref[whole * PIECE : out_rows, :].astype(F32)
    stage[merge_pieces + whole] = jnp.concatenate(
        [tail, jnp.zeros((PIECE - rest, channels), F32)], axis=0
    ).astype(BF16)

    load.wait()

    def total(i, carry):
        part = x[pl.ds(pl.multiple_of(i * 64, 64), 64), :].astype(F32)
        return carry + fold_rows(part)

    zeros = jnp.zeros((ROWS, channels), F32)
    summed = lax.fori_loop(0, rows // 64, total, zeros)
    average = group_mean(jnp.sum(summed, axis=0, keepdims=True), collect, spread, members)

    pl.semaphore_wait(barrier, shards - 1 + xs - 1 + 1)

    def beside(dz):
        return y * zs + (z + dz + zs) % zs

    pltpu.make_async_copy(stage.at[g], full.at[s, g], wr_sem.at[0]).start()
    for dz in (-2, 2, -1, 1):
        weight_copy(stage.at[g], full.at[s, g], 0, (g, beside(dz))).start()

    def total_square(i, carry):
        part = x[pl.ds(pl.multiple_of(i * 64, 64), 64), :].astype(F32) - average
        return carry + fold_rows(part * part)

    summed = lax.fori_loop(0, rows // 64, total_square, zeros)
    variance = group_mean(jnp.sum(summed, axis=0, keepdims=True), collect, spread, members)
    stats[0:1, :] = average
    fetches[2].wait()
    fetches[3].wait()
    stats[1:2, :] = lax.rsqrt(variance + 1e-05) * params[0:1, :]
    stats[2:3, :] = params[1:2, :]

    def own_slice(source, target, chunk, recv_sem):
        pltpu.make_async_copy(source.at[chunk, s], target.at[chunk, s], recv_sem.at[chunk]).start()

    def exchange(source, target, chunk, send_sem, recv_sem, start, stop):
        @pl.loop(start, stop)
        def _(step):
            to = peer_of(step)
            pltpu.make_async_remote_copy(
                src_ref=source.at[chunk, to], dst_ref=target.at[chunk, s],
                send_sem=send_sem.at[chunk], recv_sem=recv_sem.at[chunk],
                device_id=(g, to), device_id_type=MESH,
            ).start()

    def hide(chunk):
        @pl.loop(0, strips // 2)
        def _(pair):
            for side in range(halves):
                lanes = pl.ds(pl.multiple_of(side * half + chunk * LANES, LANES), LANES)
                average = stats[0:1, lanes]
                scale = stats[1:2, lanes]
                shift = stats[2:3, lanes]
                upper, lower = [], []
                for block in range(blocks):
                    at = pl.ds(pl.multiple_of(block * BLOCK + pair * 16, 16), 16)
                    value = silu((x[at, lanes].astype(F32) - average) * scale + shift)
                    upper.append(value[0:ROWS])
                    lower.append(value[ROWS : 2 * ROWS])
                send1[chunk, side * strips + 2 * pair] = jnp.concatenate(upper, axis=0).astype(BF16)
                send1[chunk, side * strips + 2 * pair + 1] = jnp.concatenate(lower, axis=0).astype(BF16)

    hide(0)
    early = shards // 4
    own_slice(send1, recv1, 0, r1_sem)
    exchange(send1, recv1, 0, s1_sem, r1_sem, 0, early)

    drain(full.at[pl.ds(0, 5), 0], wr_sem.at[0])
    way = 1 - 2 * core
    onward = full.at[beside(-2 * way), g]
    weight_copy(onward, onward, 4, (g, beside(2 * way))).start()
    for dz in (-1, 1):
        onward = full.at[beside(-2 * dz), g]
        weight_copy(onward, onward, 4, (g, beside(dz))).start()

    exchange(send1, recv1, 0, s1_sem, r1_sem, early, shards - 1)

    @pl.loop(1, chunks)
    def _(chunk):
        hide(chunk)
        own_slice(send1, recv1, chunk, r1_sem)
        exchange(send1, recv1, chunk, s1_sem, r1_sem, 0, shards - 1)

    drain(full.at[pl.ds(0, 3), 0], wr_sem.at[4])
    mine = full.at[pl.ds(y * zs, zs), g]
    for step in range(ys - 1):
        dy = zigzag(ys // 2, step)
        weight_copy(mine, mine, 1, (g, ((y + dy) % ys) * zs + z)).start()

    def gather(chunk):
        drain(recv1.at[chunk], r1_sem.at[chunk])

        @pl.loop(0, shards)
        def _(view):
            table[pl.ds(view * blocks, blocks)] = recv1[chunk, view].astype(F32).reshape(blocks, ROWS, LANES)

        @pl.loop(0, shards)
        def _(view):
            parts = []
            for block in range(blocks):
                k = view * blocks + block
                count = count_ref[k]
                second = jnp.where(count > 1, 1.0, 0.0).astype(F32)
                third = jnp.where(count > 2, 1.0, 0.0).astype(F32)
                share = jnp.where(count > 2, 1.0 / 3.0, jnp.where(count > 1, 0.5, 1.0)).astype(F32)
                value = table[src_ref[0, k]] + table[src_ref[1, k]] * second + table[src_ref[2, k]] * third
                parts.append(value * share)
            send2[chunk, view] = jnp.concatenate(parts, axis=0).astype(BF16)

        own_slice(send2, recv2, chunk, r2_sem)
        exchange(send2, recv2, chunk, s2_sem, r2_sem, 0, shards - 1)

    fetches[4].wait()
    fetches[5].wait()
    gather(0)

    drain(full.at[pl.ds(0, (ys - 1) * zs), 0], wr_sem.at[1])
    mine = full.at[:, g]
    for step in range(xs - 1):
        dx = zigzag(xs // 2, step)
        weight_copy(mine, mine, 2, (((xx + dx) % xs) * cores + core, s)).start()
    weight_copy(mine, mine, 3, (sibling, s)).start()

    @pl.loop(1, chunks)
    def _(chunk):
        gather(chunk)

    drain(full.at[pl.ds(0, (xs - 1) * shards // pieces)], wr_sem.at[2])
    for dx in range(1, xs):
        theirs = full.at[:, ((xx + dx) % xs) * cores + core]
        weight_copy(theirs, theirs, 3, (sibling, s)).start()
    drain(full.at[pl.ds(0, xs * shards // pieces)], wr_sem.at[3])

    @pl.loop(0, shards)
    def _(shard):
        for piece in range(merge_pieces):
            at = pl.ds(pl.multiple_of(shard * merge_rows + piece * PIECE, PIECE), PIECE)
            merge_w[at, :] = full[shard, piece]

    @pl.loop(0, shards // 2)
    def _(pair):
        parts = []
        for member in range(2):
            for piece in range(whole + 1):
                part = full[2 * pair + member, merge_pieces + piece].astype(F32)
                parts.append(part if piece < whole else part[0:rest])
        at = pl.ds(pl.multiple_of(pair * 2 * out_rows, PIECE), 2 * out_rows)
        out_w[at, :] = jnp.concatenate(parts, axis=0).astype(BF16)

    tile = 256
    tile_strips = tile // slice_rows
    tiles = rows // tile

    def left(ref, chunk_list, side, m):
        at = pl.ds(side * strips + m * tile_strips, tile_strips)
        return jnp.concatenate([ref[chunk, at].reshape(tile, LANES) for chunk in chunk_list], axis=1)

    @pl.loop(0, tiles)
    def _(m):
        sides = [left(send1, range(chunks), side, m) for side in range(halves)]
        at = pl.ds(pl.multiple_of(m * tile, tile), tile)
        acc[at, :] = jnp.dot(
            jnp.concatenate(sides, axis=1), merge_w[0:channels, :], preferred_element_type=F32
        )

    def add_epipolar(chunk_list, m):
        depth = len(chunk_list) * LANES
        first = chunk_list[0] * LANES
        sides = [left(recv2, chunk_list, side, m) for side in range(halves)]
        weights = [
            merge_w[channels + side * half + first : channels + side * half + first + depth, :]
            for side in range(halves)
        ]
        at = pl.ds(pl.multiple_of(m * tile, tile), tile)
        value = acc[at, :] + jnp.dot(
            jnp.concatenate(sides, axis=1), jnp.concatenate(weights, axis=0), preferred_element_type=F32
        )
        acc[at, :] = value
        return value

    first = 0
    while first < chunks - 1:
        group = list(range(first, min(first + 2, chunks - 1)))
        for chunk in group:
            drain(recv2.at[chunk], r2_sem.at[chunk])

        @pl.loop(0, tiles)
        def _(m):
            add_epipolar(group, m)

        first += len(group)

    def partial(i, carry):
        return carry + fold_rows(acc[pl.ds(pl.multiple_of(i * 64, 64), 64), :])

    summed = lax.fori_loop(0, rows // 64, partial, zeros)
    stats[0:1, :] = group_mean(jnp.sum(summed, axis=0, keepdims=True), collect, spread, members)

    drain(recv2.at[chunks - 1], r2_sem.at[chunks - 1])

    width = 256
    spans = channels // width
    lasts = [left(recv2, [chunks - 1], side, m) for m in range(tiles) for side in range(halves)]
    first = (chunks - 1) * LANES
    sums = []
    for n in range(spans):
        columns = slice(n * width, (n + 1) * width)
        weights = [
            merge_w[channels + side * half + first : channels + side * half + first + LANES, columns]
            for side in range(halves)
        ]
        weights = jnp.concatenate(weights, axis=0)
        middle = stats[0:1, columns]
        summed = jnp.zeros((ROWS, width), F32)
        squares = jnp.zeros((ROWS, width), F32)
        for m in range(tiles):
            at = slice(m * tile, (m + 1) * tile)
            inputs = jnp.concatenate(lasts[halves * m : halves * (m + 1)], axis=1)
            difference = acc[at, columns] - middle + jnp.dot(inputs, weights, preferred_element_type=F32)
            acc[at, columns] = difference
            summed = summed + fold_rows(difference)
            squares = squares + fold_rows(difference * difference)
        sums.append((summed, squares))
    rows_of = [
        jnp.sum(jnp.concatenate([pair[i] for pair in sums], axis=1), axis=0, keepdims=True) for i in range(2)
    ]
    moved, square = [total / members for total in exact_rows(rows_of, collect)]
    scale = lax.rsqrt(jnp.maximum(square - moved * moved, 0.0) + 1e-05)
    moved, scale = exact_rows([moved, scale], spread)
    stats[0:1, :] = moved
    stats[1:2, :] = scale

    for chunk in range(chunks):
        drain(send1.at[chunk, pl.ds(0, shards - 1)], s1_sem.at[chunk])
        drain(send2.at[chunk, pl.ds(0, shards - 1)], s2_sem.at[chunk])
    drain(full.at[pl.ds(0, 4), 0], ws_sem.at[0])
    drain(full.at[pl.ds(0, 3), 0], ws_sem.at[4])
    drain(full.at[pl.ds(0, (ys - 1) * zs), 0], ws_sem.at[1])
    drain(full.at[pl.ds(0, (xs - 1) * shards // pieces)], ws_sem.at[2])
    drain(full.at[pl.ds(0, xs * shards // pieces)], ws_sem.at[3])


def finish(x_ref, out_w, acc, stats, out_hbm, act, result, sem):
    rows, channels = acc.shape
    blocks = rows // BLOCK
    slice_rows = blocks * ROWS
    tile = width = 256
    tile_strips = tile // slice_rows
    tiles, spans = rows // tile, channels // width

    def activate(m, n):
        at, columns = slice(m * tile, (m + 1) * tile), slice(n * width, (n + 1) * width)
        value = silu((acc[at, columns] - stats[0:1, columns]) * stats[1:2, columns])
        act[at, columns] = value.astype(BF16)

    for n in range(spans):
        activate(0, n)
    for m in range(tiles):
        at = slice(m * tile, (m + 1) * tile)
        for n in range(spans):
            columns = slice(n * width, (n + 1) * width)
            projected = jnp.dot(act[at, :], out_w[:, columns], preferred_element_type=F32)
            if m + 1 < tiles:
                activate(m + 1, n)
            for pair in range(tile_strips // 2):
                top = 2 * pair * slice_rows
                for block in range(blocks):
                    upper = projected[top + block * ROWS : top + (block + 1) * ROWS]
                    lower = projected[top + slice_rows + block * ROWS : top + slice_rows + (block + 1) * ROWS]
                    start = block * BLOCK + m * (tile_strips * ROWS) + pair * 2 * ROWS
                    to = slice(start, start + 2 * ROWS)
                    value = x_ref[to, columns].astype(F32) + jnp.concatenate([upper, lower], axis=0)
                    result[to, columns] = value.astype(BF16)
        for block in range(blocks):
            to = pl.ds(block * BLOCK + m * (tile_strips * ROWS), tile_strips * ROWS)
            pltpu.make_async_copy(result.at[to], out_hbm.at[to], sem).start()
    pltpu.make_async_copy(result, out_hbm, sem).wait()


def solution(mesh):
    sizes = (4, 8, 4, 2)

    def per_device(features, norm_gain, norm_shift, merge_weight, out_weight, corr_src, corr_count):
        rows, channels = features.shape
        shards = lax.axis_size("shard")
        groups = lax.axis_size("grp")
        slice_rows = rows // BLOCK * ROWS
        chunks = channels // (shards // (BLOCK // ROWS)) // LANES
        hbm = pl.BlockSpec(memory_space=pltpu.HBM)
        slices = pltpu.VMEM((chunks, shards, slice_rows, LANES), BF16)
        dma = pltpu.SemaphoreType.DMA
        vmem = pl.BlockSpec(memory_space=pltpu.VMEM)
        whole = pltpu.VMEM(features.shape, BF16)
        handed = pl.pallas_call(
            functools.partial(kernel, sizes),
            out_shape=[
                whole,
                pltpu.VMEM((channels, channels), BF16),
                pltpu.VMEM((rows, channels), F32),
                pltpu.VMEM((ROWS, channels), F32),
            ],
            in_specs=[hbm] * 7,
            out_specs=[vmem] * 4,
            scratch_shapes=[
                pltpu.VMEM((ROWS, channels), F32),
                pltpu.VMEM(merge_weight.shape, BF16),
                pltpu.VMEM(out_weight.shape, BF16),
                pltpu.SMEM(corr_src.shape[::-1], jnp.int32),
                pltpu.SMEM(corr_count.shape, jnp.int32),
                pltpu.VMEM((groups, PIECE, channels), BF16),
                slices, slices, slices, slices,
                pltpu.VMEM((corr_src.shape[0], ROWS, LANES), F32),
                pltpu.VMEM((shards, groups, PIECE, channels), BF16),
                pltpu.VMEM((2 * channels, channels), BF16),
                pltpu.VMEM((channels, LANES), BF16),
                pltpu.VMEM((LANES, channels), BF16),
                dma((7,)),
                dma((chunks,)), dma((chunks,)), dma((chunks,)), dma((chunks,)),
                dma((5,)), dma((5,)),
            ],
            compiler_params=pltpu.CompilerParams(
                collective_id=0, has_side_effects=True, vmem_limit_bytes=42 * 1024 * 1024
            ),
            name="merge_block",
        )(
            *(
                pltpu.with_memory_space_constraint(array, pltpu.HBM)
                for array in (
                    features, norm_gain, norm_shift, merge_weight, out_weight, corr_src.T, corr_count
                )
            )
        )
        return pl.pallas_call(
            finish,
            out_shape=jax.ShapeDtypeStruct(features.shape, features.dtype),
            in_specs=[vmem] * 4,
            out_specs=pl.BlockSpec(memory_space=pl.ANY),
            scratch_shapes=[whole, whole, dma],
            compiler_params=pltpu.CompilerParams(vmem_limit_bytes=20 * 1024 * 1024),
            name="finish_block",
        )(*handed)

    placed = (
        P(("grp", "shard"), None),
        P(),
        P(),
        P("shard", None),
        P("shard", None),
        P("grp", None),
        P("grp"),
    )
    return jax.shard_map(
        per_device, mesh=mesh, in_specs=placed, out_specs=P(("grp", "shard"), None), check_vma=False
    )
```

```python
import functools

import jax
import jax.numpy as jnp
from jax import lax
from jax.experimental import pallas as pl
from jax.experimental.pallas import tpu as pltpu
from jax.sharding import PartitionSpec as P

GROUPS = 32
BLOCK = 128
LANES = 128
ROWS = 8
PIECE = 16
MESH = pl.DeviceIdType.MESH
F32 = jnp.float32
BF16 = jnp.bfloat16


def zigzag(center, place):
    odd = place % 2
    return center + (1 - odd) * (place // 2) - odd * ((place + 1) // 2)


def exact_rows(rows, matrix):
    parts = []
    for row in rows:
        high = row.astype(BF16).astype(F32)
        rest = row - high
        middle = rest.astype(BF16).astype(F32)
        parts += [high, middle, rest - middle]
    parts.append(jnp.zeros((PIECE - len(parts), rows[0].shape[1]), F32))
    stacked = jnp.concatenate(parts, axis=0).astype(BF16)
    product = jnp.dot(stacked, matrix[...], preferred_element_type=F32)
    return [product[i : i + 1] + product[i + 1 : i + 2] + product[i + 2 : i + 3] for i in range(0, 3 * len(rows), 3)]


def group_mean(row, collect, spread, members):
    (total,) = exact_rows([row], collect)
    return exact_rows([total / members], spread)[0]


def fold_rows(values):
    return jnp.sum(values.reshape(values.shape[0] // ROWS, ROWS, values.shape[1]), axis=0)


def silu(values):
    middle = 0.5 * values
    return middle + middle * jnp.tanh(middle)


def kernel(
    sizes,
    x_hbm, gain_hbm, shift_hbm, merge_hbm, outw_hbm, src_hbm, count_hbm,
    x, out_w, acc, stats,
    params, merge_ref, outw_ref, src_ref, count_ref, stage, send1, recv1, send2, recv2, table, full, merge_w, collect, spread,
    load_sem, s1_sem, r1_sem, s2_sem, r2_sem, ws_sem, wr_sem,
):
    ys, zs, xs, cores = sizes
    shards = ys * zs
    rows, channels = x.shape
    blocks = rows // BLOCK
    strips = BLOCK // ROWS
    halves = shards // strips
    half = channels // halves
    chunks = half // LANES
    pieces = full.shape[1]
    merge_rows = merge_ref.shape[0]
    out_rows = outw_ref.shape[0]
    merge_pieces = merge_rows // PIECE
    group_width = channels // GROUPS
    members = float(rows * group_width)
    slice_rows = blocks * ROWS

    s = lax.axis_index("shard")
    g = lax.axis_index("grp")
    y, z = s // zs, s % zs
    xx, core = g // cores, g % cores

    load = pltpu.make_async_copy(x_hbm, x, load_sem.at[0])
    load.start()
    fetches = [
        pltpu.make_async_copy(source, target, load_sem.at[1 + i])
        for i, (source, target) in enumerate(
            (
                (merge_hbm, merge_ref), (outw_hbm, outw_ref), (gain_hbm, params.at[0]), (shift_hbm, params.at[1]),
                (src_hbm, src_ref), (count_hbm, count_ref),
            )
        )
    ]
    for fetch in fetches:
        fetch.start()

    def peer_of(step):
        dz = zigzag(zs // 2, step // ys)
        dy = zigzag(ys // 2, step % ys)
        return ((y + dy) % ys) * zs + (z + dz) % zs

    barrier = pltpu.get_barrier_semaphore()

    @pl.loop(0, shards - 1)
    def _(step):
        pl.semaphore_signal(barrier, inc=1, device_id=(g, peer_of(step)), device_id_type=MESH)

    for dx in range(1, xs):
        to = ((xx + dx) % xs) * cores + core
        pl.semaphore_signal(barrier, inc=1, device_id=(to, s), device_id_type=MESH)
    sibling = xx * cores + (core + 1) % cores
    pl.semaphore_signal(barrier, inc=1, device_id=(sibling, s), device_id_type=MESH)

    lane = lax.broadcasted_iota(jnp.int32, (channels, LANES), 1) * group_width
    row = lax.broadcasted_iota(jnp.int32, (channels, LANES), 0)
    collect[...] = jnp.where((row >= lane) & (row < lane + group_width), 1.0, 0.0).astype(BF16)
    lane = lax.broadcasted_iota(jnp.int32, (LANES, channels), 1)
    row = lax.broadcasted_iota(jnp.int32, (LANES, channels), 0) * group_width
    spread[...] = jnp.where((lane >= row) & (lane < row + group_width), 1.0, 0.0).astype(BF16)

    def weight_copy(source, target, stage_no, to):
        return pltpu.make_async_remote_copy(
            src_ref=source, dst_ref=target, send_sem=ws_sem.at[stage_no], recv_sem=wr_sem.at[stage_no],
            device_id=to, device_id_type=MESH,
        )

    def drain(ref, sem):
        pltpu.make_async_copy(ref, ref, sem).wait()

    fetches[0].wait()
    fetches[1].wait()

    for piece in range(merge_pieces):
        stage[piece] = merge_ref[piece * PIECE : (piece + 1) * PIECE, :]
    whole = out_rows // PIECE
    for piece in range(whole):
        stage[merge_pieces + piece] = outw_ref[piece * PIECE : (piece + 1) * PIECE, :]
    rest = out_rows - whole * PIECE
    tail = outw_ref[whole * PIECE : out_rows, :].astype(F32)
    stage[merge_pieces + whole] = jnp.concatenate(
        [tail, jnp.zeros((PIECE - rest, channels), F32)], axis=0
    ).astype(BF16)

    load.wait()

    def total(i, carry):
        part = x[pl.ds(pl.multiple_of(i * 64, 64), 64), :].astype(F32)
        return carry + fold_rows(part)

    zeros = jnp.zeros((ROWS, channels), F32)
    summed = lax.fori_loop(0, rows // 64, total, zeros)
    average = group_mean(jnp.sum(summed, axis=0, keepdims=True), collect, spread, members)

    pl.semaphore_wait(barrier, shards - 1 + xs - 1 + 1)

    def beside(dz):
        return y * zs + (z + dz + zs) % zs

    pltpu.make_async_copy(stage.at[g], full.at[s, g], wr_sem.at[0]).start()
    for dz in (-2, 2, -1, 1):
        weight_copy(stage.at[g], full.at[s, g], 0, (g, beside(dz))).start()

    def total_square(i, carry):
        part = x[pl.ds(pl.multiple_of(i * 64, 64), 64), :].astype(F32) - average
        return carry + fold_rows(part * part)

    summed = lax.fori_loop(0, rows // 64, total_square, zeros)
    variance = group_mean(jnp.sum(summed, axis=0, keepdims=True), collect, spread, members)
    stats[0:1, :] = average
    fetches[2].wait()
    fetches[3].wait()
    stats[1:2, :] = lax.rsqrt(variance + 1e-05) * params[0:1, :]
    stats[2:3, :] = params[1:2, :]

    def own_slice(source, target, chunk, recv_sem):
        pltpu.make_async_copy(source.at[chunk, s], target.at[chunk, s], recv_sem.at[chunk]).start()

    def exchange(source, target, chunk, send_sem, recv_sem, start, stop):
        @pl.loop(start, stop)
        def _(step):
            to = peer_of(step)
            pltpu.make_async_remote_copy(
                src_ref=source.at[chunk, to], dst_ref=target.at[chunk, s],
                send_sem=send_sem.at[chunk], recv_sem=recv_sem.at[chunk],
                device_id=(g, to), device_id_type=MESH,
            ).start()

    def hide(chunk):
        @pl.loop(0, strips // 2)
        def _(pair):
            for side in range(halves):
                lanes = pl.ds(pl.multiple_of(side * half + chunk * LANES, LANES), LANES)
                average = stats[0:1, lanes]
                scale = stats[1:2, lanes]
                shift = stats[2:3, lanes]
                upper, lower = [], []
                for block in range(blocks):
                    at = pl.ds(pl.multiple_of(block * BLOCK + pair * 16, 16), 16)
                    value = silu((x[at, lanes].astype(F32) - average) * scale + shift)
                    upper.append(value[0:ROWS])
                    lower.append(value[ROWS : 2 * ROWS])
                send1[chunk, side * strips + 2 * pair] = jnp.concatenate(upper, axis=0).astype(BF16)
                send1[chunk, side * strips + 2 * pair + 1] = jnp.concatenate(lower, axis=0).astype(BF16)

    hide(0)
    early = shards // 4
    own_slice(send1, recv1, 0, r1_sem)
    exchange(send1, recv1, 0, s1_sem, r1_sem, 0, early)

    drain(full.at[pl.ds(0, 5), 0], wr_sem.at[0])
    way = 1 - 2 * core
    onward = full.at[beside(-2 * way), g]
    weight_copy(onward, onward, 4, (g, beside(2 * way))).start()
    for dz in (-1, 1):
        onward = full.at[beside(-2 * dz), g]
        weight_copy(onward, onward, 4, (g, beside(dz))).start()

    exchange(send1, recv1, 0, s1_sem, r1_sem, early, shards - 1)

    @pl.loop(1, chunks)
    def _(chunk):
        hide(chunk)
        own_slice(send1, recv1, chunk, r1_sem)
        exchange(send1, recv1, chunk, s1_sem, r1_sem, 0, shards - 1)

    drain(full.at[pl.ds(0, 3), 0], wr_sem.at[4])
    mine = full.at[pl.ds(y * zs, zs), g]
    for step in range(ys - 1):
        dy = zigzag(ys // 2, step)
        weight_copy(mine, mine, 1, (g, ((y + dy) % ys) * zs + z)).start()

    def gather(chunk):
        drain(recv1.at[chunk], r1_sem.at[chunk])

        @pl.loop(0, shards)
        def _(view):
            table[pl.ds(view * blocks, blocks)] = recv1[chunk, view].astype(F32).reshape(blocks, ROWS, LANES)

        @pl.loop(0, shards)
        def _(view):
            parts = []
            for block in range(blocks):
                k = view * blocks + block
                count = count_ref[k]
                second = jnp.where(count > 1, 1.0, 0.0).astype(F32)
                third = jnp.where(count > 2, 1.0, 0.0).astype(F32)
                share = jnp.where(count > 2, 1.0 / 3.0, jnp.where(count > 1, 0.5, 1.0)).astype(F32)
                value = table[src_ref[0, k]] + table[src_ref[1, k]] * second + table[src_ref[2, k]] * third
                parts.append(value * share)
            send2[chunk, view] = jnp.concatenate(parts, axis=0).astype(BF16)

        own_slice(send2, recv2, chunk, r2_sem)
        exchange(send2, recv2, chunk, s2_sem, r2_sem, 0, shards - 1)

    fetches[4].wait()
    fetches[5].wait()
    gather(0)

    drain(full.at[pl.ds(0, (ys - 1) * zs), 0], wr_sem.at[1])
    mine = full.at[:, g]
    for step in range(xs - 1):
        dx = zigzag(xs // 2, step)
        weight_copy(mine, mine, 2, (((xx + dx) % xs) * cores + core, s)).start()
    weight_copy(mine, mine, 3, (sibling, s)).start()

    @pl.loop(1, chunks)
    def _(chunk):
        gather(chunk)

    drain(full.at[pl.ds(0, (xs - 1) * shards // pieces)], wr_sem.at[2])
    for dx in range(1, xs):
        theirs = full.at[:, ((xx + dx) % xs) * cores + core]
        weight_copy(theirs, theirs, 3, (sibling, s)).start()
    drain(full.at[pl.ds(0, xs * shards // pieces)], wr_sem.at[3])

    @pl.loop(0, shards)
    def _(shard):
        for piece in range(merge_pieces):
            at = pl.ds(pl.multiple_of(shard * merge_rows + piece * PIECE, PIECE), PIECE)
            merge_w[at, :] = full[shard, piece]

    @pl.loop(0, shards // 2)
    def _(pair):
        parts = []
        for member in range(2):
            for piece in range(whole + 1):
                part = full[2 * pair + member, merge_pieces + piece].astype(F32)
                parts.append(part if piece < whole else part[0:rest])
        at = pl.ds(pl.multiple_of(pair * 2 * out_rows, PIECE), 2 * out_rows)
        out_w[at, :] = jnp.concatenate(parts, axis=0).astype(BF16)

    tile = 256
    tile_strips = tile // slice_rows
    tiles = rows // tile

    def left(ref, chunk_list, side, m):
        at = pl.ds(side * strips + m * tile_strips, tile_strips)
        return jnp.concatenate([ref[chunk, at].reshape(tile, LANES) for chunk in chunk_list], axis=1)

    @pl.loop(0, tiles)
    def _(m):
        sides = [left(send1, range(chunks), side, m) for side in range(halves)]
        at = pl.ds(pl.multiple_of(m * tile, tile), tile)
        acc[at, :] = jnp.dot(
            jnp.concatenate(sides, axis=1), merge_w[0:channels, :], preferred_element_type=F32
        )

    def add_epipolar(chunk_list, m):
        depth = len(chunk_list) * LANES
        first = chunk_list[0] * LANES
        sides = [left(recv2, chunk_list, side, m) for side in range(halves)]
        weights = [
            merge_w[channels + side * half + first : channels + side * half + first + depth, :]
            for side in range(halves)
        ]
        at = pl.ds(pl.multiple_of(m * tile, tile), tile)
        value = acc[at, :] + jnp.dot(
            jnp.concatenate(sides, axis=1), jnp.concatenate(weights, axis=0), preferred_element_type=F32
        )
        acc[at, :] = value
        return value

    first = 0
    while first < chunks - 1:
        group = list(range(first, min(first + 2, chunks - 1)))
        for chunk in group:
            drain(recv2.at[chunk], r2_sem.at[chunk])

        @pl.loop(0, tiles)
        def _(m):
            add_epipolar(group, m)

        first += len(group)

    def partial(i, carry):
        return carry + fold_rows(acc[pl.ds(pl.multiple_of(i * 64, 64), 64), :])

    summed = lax.fori_loop(0, rows // 64, partial, zeros)
    stats[0:1, :] = group_mean(jnp.sum(summed, axis=0, keepdims=True), collect, spread, members)

    drain(recv2.at[chunks - 1], r2_sem.at[chunks - 1])

    width = 256
    spans = channels // width
    lasts = [left(recv2, [chunks - 1], side, m) for m in range(tiles) for side in range(halves)]
    first = (chunks - 1) * LANES
    sums = []
    for n in range(spans):
        columns = slice(n * width, (n + 1) * width)
        weights = [
            merge_w[channels + side * half + first : channels + side * half + first + LANES, columns]
            for side in range(halves)
        ]
        weights = jnp.concatenate(weights, axis=0)
        middle = stats[0:1, columns]
        summed = jnp.zeros((ROWS, width), F32)
        squares = jnp.zeros((ROWS, width), F32)
        for m in range(tiles):
            at = slice(m * tile, (m + 1) * tile)
            inputs = jnp.concatenate(lasts[halves * m : halves * (m + 1)], axis=1)
            difference = acc[at, columns] - middle + jnp.dot(inputs, weights, preferred_element_type=F32)
            acc[at, columns] = difference
            summed = summed + fold_rows(difference)
            squares = squares + fold_rows(difference * difference)
        sums.append((summed, squares))
    rows_of = [
        jnp.sum(jnp.concatenate([pair[i] for pair in sums], axis=1), axis=0, keepdims=True) for i in range(2)
    ]
    moved, square = [total / members for total in exact_rows(rows_of, collect)]
    scale = lax.rsqrt(jnp.maximum(square - moved * moved, 0.0) + 1e-05)
    moved, scale = exact_rows([moved, scale], spread)
    stats[0:1, :] = moved
    stats[1:2, :] = scale

    for chunk in range(chunks):
        drain(send1.at[chunk, pl.ds(0, shards - 1)], s1_sem.at[chunk])
        drain(send2.at[chunk, pl.ds(0, shards - 1)], s2_sem.at[chunk])
    drain(full.at[pl.ds(0, 4), 0], ws_sem.at[0])
    drain(full.at[pl.ds(0, 3), 0], ws_sem.at[4])
    drain(full.at[pl.ds(0, (ys - 1) * zs), 0], ws_sem.at[1])
    drain(full.at[pl.ds(0, (xs - 1) * shards // pieces)], ws_sem.at[2])
    drain(full.at[pl.ds(0, xs * shards // pieces)], ws_sem.at[3])


def finish(x_ref, out_w, acc, stats, out_hbm, act, result, sem):
    rows, channels = acc.shape
    blocks = rows // BLOCK
    slice_rows = blocks * ROWS
    tile = width = 256
    tile_strips = tile // slice_rows
    tiles, spans = rows // tile, channels // width

    def activate(m, n):
        at, columns = slice(m * tile, (m + 1) * tile), slice(n * width, (n + 1) * width)
        value = silu((acc[at, columns] - stats[0:1, columns]) * stats[1:2, columns])
        act[at, columns] = value.astype(BF16)

    for n in range(spans):
        activate(0, n)
    for m in range(tiles):
        at = slice(m * tile, (m + 1) * tile)
        sent = 0
        for n in range(spans):
            columns = slice(n * width, (n + 1) * width)
            projected = jnp.dot(act[at, :], out_w[:, columns], preferred_element_type=F32)
            if m + 1 < tiles:
                activate(m + 1, n)
            for pair in range(tile_strips // 2):
                top = 2 * pair * slice_rows
                for block in range(blocks):
                    upper = projected[top + block * ROWS : top + (block + 1) * ROWS]
                    lower = projected[top + slice_rows + block * ROWS : top + slice_rows + (block + 1) * ROWS]
                    start = block * BLOCK + m * (tile_strips * ROWS) + pair * 2 * ROWS
                    to = slice(start, start + 2 * ROWS)
                    value = x_ref[to, columns].astype(F32) + jnp.concatenate([upper, lower], axis=0)
                    inside = slice(start - block * BLOCK, start - block * BLOCK + 2 * ROWS)
                    result[block, inside, columns] = value.astype(BF16)
            if n in (2, spans - 1):
                rows_of = pl.ds(m * tile_strips * ROWS, tile_strips * ROWS)
                columns = pl.ds(sent * width, (n + 1 - sent) * width)
                pltpu.make_async_copy(
                    result.at[:, rows_of, columns], out_hbm.at[:, rows_of, columns], sem
                ).start()
                sent = n + 1
    pltpu.make_async_copy(result, out_hbm, sem).wait()


def solution(mesh):
    sizes = (4, 8, 4, 2)

    def per_device(features, norm_gain, norm_shift, merge_weight, out_weight, corr_src, corr_count):
        rows, channels = features.shape
        shards = lax.axis_size("shard")
        groups = lax.axis_size("grp")
        slice_rows = rows // BLOCK * ROWS
        chunks = channels // (shards // (BLOCK // ROWS)) // LANES
        hbm = pl.BlockSpec(memory_space=pltpu.HBM)
        slices = pltpu.VMEM((chunks, shards, slice_rows, LANES), BF16)
        dma = pltpu.SemaphoreType.DMA
        vmem = pl.BlockSpec(memory_space=pltpu.VMEM)
        whole = pltpu.VMEM(features.shape, BF16)
        handed = pl.pallas_call(
            functools.partial(kernel, sizes),
            out_shape=[
                whole,
                pltpu.VMEM((channels, channels), BF16),
                pltpu.VMEM((rows, channels), F32),
                pltpu.VMEM((ROWS, channels), F32),
            ],
            in_specs=[hbm] * 7,
            out_specs=[vmem] * 4,
            scratch_shapes=[
                pltpu.VMEM((ROWS, channels), F32),
                pltpu.VMEM(merge_weight.shape, BF16),
                pltpu.VMEM(out_weight.shape, BF16),
                pltpu.SMEM(corr_src.shape[::-1], jnp.int32),
                pltpu.SMEM(corr_count.shape, jnp.int32),
                pltpu.VMEM((groups, PIECE, channels), BF16),
                slices, slices, slices, slices,
                pltpu.VMEM((corr_src.shape[0], ROWS, LANES), F32),
                pltpu.VMEM((shards, groups, PIECE, channels), BF16),
                pltpu.VMEM((2 * channels, channels), BF16),
                pltpu.VMEM((channels, LANES), BF16),
                pltpu.VMEM((LANES, channels), BF16),
                dma((7,)),
                dma((chunks,)), dma((chunks,)), dma((chunks,)), dma((chunks,)),
                dma((5,)), dma((5,)),
            ],
            compiler_params=pltpu.CompilerParams(
                collective_id=0, has_side_effects=True, vmem_limit_bytes=42 * 1024 * 1024
            ),
            name="merge_block",
        )(
            *(
                pltpu.with_memory_space_constraint(array, pltpu.HBM)
                for array in (
                    features, norm_gain, norm_shift, merge_weight, out_weight, corr_src.T, corr_count
                )
            )
        )
        blocked = (rows // BLOCK, BLOCK, channels)
        return pl.pallas_call(
            finish,
            out_shape=jax.ShapeDtypeStruct(blocked, features.dtype),
            in_specs=[vmem] * 4,
            out_specs=pl.BlockSpec(memory_space=pl.ANY),
            scratch_shapes=[whole, pltpu.VMEM(blocked, BF16), dma],
            compiler_params=pltpu.CompilerParams(vmem_limit_bytes=20 * 1024 * 1024),
            name="finish_block",
        )(*handed).reshape(features.shape)

    placed = (
        P(("grp", "shard"), None),
        P(),
        P(),
        P("shard", None),
        P("shard", None),
        P("grp", None),
        P("grp"),
    )
    return jax.shard_map(
        per_device, mesh=mesh, in_specs=placed, out_specs=P(("grp", "shard"), None), check_vma=False
    )
```
